256 devices in a mesh: row: 32 (over y, z_hi, core), col: 8 (over x, z_lo).
Axes of the slice: x: 4, y: 4, z: 8 (z_hi: 4, z_lo: 2; z = z_hi * 2 + z_lo), core: 2. Of those that a mesh axis runs over, the one named last changes fastest.
Arguments:
- features: bfloat16 [32768, 512], P(('row', 'col')), may hold values from -6 to 6
- degrees: int32 [32768], P(('row', 'col')), may hold values from 768 to 1535
- tile_rows: int32 [32, 8, 32, 3], P('row', 'col'), may hold values from 0 to 7
- tile_masks: int32 [32, 8, 32, 3, 128, 128], P('row', 'col'), may hold values 0 or 1
- w_self: bfloat16 [512, 512], replicated, may hold values from -0.25 to 0.25
- w_neigh: bfloat16 [512, 512], replicated, may hold values from -6 to 6
- bias: float32 [512], replicated, may hold values from -3 to 3
- cotangent: bfloat16 [32768, 512], P(('row', 'col')), may hold values from -6 to 6
Outputs:
- output: bfloat16 [32768, 512], P(('row', 'col'))
- grad_features: bfloat16 [32768, 512], P(('row', 'col'))
The draws below stay inside these ranges and needn't reach their ends.
All inputs are finite; a program needn't handle non-finite values. No bound on the sum of `tile_masks` on one device may be relied on, other than what follows from the above.
Results may differ from the reference program's by a relative error of at most 0.024.
Values may be sent and summed in bfloat16 or wider, within the bound.
No kernel may reach another device: no remote copies, remote signals or barrier semaphores. Data moves between devices by JAX's collectives and lax.ppermute only.
A program may use at most 128 MiB of HBM per device.

```python
import jax
import jax.numpy as jnp
from jax import lax

F = 512
TILE = 128
SLOTS = 3
NODES = 32768
TROWS = 8
TCOLS = 32
DEG_LO = 768
N_ROW = 32
N_COL = 8


def touch_ends(values, own_key, smallest, largest):
    place = [jax.random.randint(jax.random.fold_in(own_key, axis), (), 0, length) for axis, length in enumerate(values.shape)]
    widest = values.shape.index(max(values.shape))
    neighbour = place[:widest] + [(place[widest] + 1) % values.shape[widest]] + place[widest + 1:]
    return values.at[tuple(place)].set(smallest).at[tuple(neighbour)].set(largest)


def block_levels(stream_key, extent, shards, smallest, high):
    level, own = 1.0, jax.random.fold_in(stream_key, 6)
    for dim, shards_of in shards:
        heights = jnp.exp(jax.random.uniform(jax.random.fold_in(own, dim), (shards_of,), jnp.float32, smallest / len(shards), high / len(shards)))
        level = level * jnp.repeat(heights, extent[dim] // shards_of).reshape([-1 if axis == dim else 1 for axis in range(len(extent))])
    return level


def bell_draw(stream_key, dims, scale, reach, shards=(), kind=jnp.bfloat16):
    level = block_levels(stream_key, dims, shards, -0.22, 0.18) if shards else 1.0
    values = jax.random.normal(stream_key, dims, jnp.float32) * scale * level
    return jnp.minimum(jnp.maximum(values, -reach), reach).astype(kind)


def setup_inputs(seed: int = 0) -> dict:
    streams_of = jax.random.split(jax.random.key(seed), 9)
    return {
        "features": bell_draw(streams_of[0], (NODES, F), 1.0, 6.0, ((0, 256),)),
        "degrees": touch_ends(jax.random.randint(streams_of[1], (NODES,), DEG_LO, 2 * DEG_LO), jax.random.fold_in(streams_of[1], 1), DEG_LO, (2 * DEG_LO) - 1).astype(jnp.int32),
        "tile_rows": touch_ends(jax.random.randint(streams_of[2], (N_ROW, N_COL, TCOLS, SLOTS), 0, TROWS), jax.random.fold_in(streams_of[2], 1), 0, TROWS - 1).astype(jnp.int32),
        "tile_masks": touch_ends((jax.random.randint(streams_of[3], (N_ROW, N_COL, TCOLS, SLOTS, TILE, TILE), 0, 16) < 1).astype(jnp.int32), jax.random.fold_in(streams_of[3], 1), 0, 1),
        "w_self": bell_draw(streams_of[4], (F, F), F ** -0.5, 0.25),
        "w_neigh": bell_draw(streams_of[5], (F, F), (1.5 * DEG_LO ** 0.5 * F ** -0.5), 6.0),
        "bias": bell_draw(streams_of[6], (F,), 0.5, 3.0, (), jnp.float32),
        "cotangent": bell_draw(streams_of[7], (NODES, F), 1.0, 6.0, ((0, 256),)),
    }


def silu_slope(pre):
    sig = jax.nn.sigmoid(pre)
    return sig * (1.0 + pre * (1.0 - sig))


def round_half(values):
    return lax.optimization_barrier(values.astype(jnp.bfloat16)).astype(jnp.float32)


def reference(features, degrees, tile_rows, tile_masks, w_self, w_neigh, bias, cotangent):
    n_row, n_col, col_tiles, slots, tile, _ = tile_masks.shape
    width = features.shape[1]
    local_nodes = features.shape[0] // (n_row * n_col)
    row_tiles = n_col * local_nodes // tile
    by_shard = features.reshape(n_row, n_col, local_nodes, width)
    highest = lax.Precision.HIGHEST

    def dest_block(r):
        def step(total, c):
            source = lax.dynamic_index_in_dim(by_shard, c, 1, keepdims=False)
            blocks = source.reshape(col_tiles, tile, width).astype(jnp.float32)
            masks = tile_masks[r, c].astype(jnp.float32)
            prods = jnp.einsum("jkuv,jvf->jkuf", masks, blocks, precision=highest)
            which = tile_rows[r, c].reshape(-1).astype(jnp.int32)
            contrib = jnp.zeros((row_tiles, tile, width), jnp.float32).at[which].add(prods.reshape(col_tiles * slots, tile, width))
            return total + round_half(contrib), None

        start = jnp.zeros((row_tiles, tile, width), jnp.float32)
        total, _ = lax.scan(step, start, jnp.arange(n_col, dtype=jnp.int32))
        return total.reshape(row_tiles * tile, width)

    summed = lax.map(dest_block, jnp.arange(n_row, dtype=jnp.int32)).reshape(-1, width)
    degf = degrees.astype(jnp.float32)
    mean_neigh = (summed / degf[:, None]).astype(jnp.bfloat16)
    pre = jnp.dot(features, w_self, preferred_element_type=jnp.float32)
    pre = pre + jnp.dot(mean_neigh, w_neigh, preferred_element_type=jnp.float32) + bias[None, :]
    output = jax.nn.silu(pre).astype(jnp.bfloat16)
    grad_pre = (cotangent.astype(jnp.float32) * silu_slope(pre)).astype(jnp.bfloat16)
    proj = lax.dot_general(grad_pre, w_neigh, (((1,), (1,)), ((), ())), preferred_element_type=jnp.float32)
    scaled = (proj / degf[:, None]).astype(jnp.bfloat16)
    spread_blocks = scaled.reshape(n_row, row_tiles, tile, width)

    def source_block(c):
        def step(total, r):
            table = lax.dynamic_index_in_dim(spread_blocks, r, 0, keepdims=False).astype(jnp.float32)
            picked = table[tile_rows[r, c]]
            masks = tile_masks[r, c].astype(jnp.float32)
            added = jnp.einsum("jkuv,jkuf->jvf", masks, picked, precision=highest)
            return total + round_half(added), None

        start = jnp.zeros((col_tiles, tile, width), jnp.float32)
        total, _ = lax.scan(step, start, jnp.arange(n_row, dtype=jnp.int32))
        return total.reshape(n_row, local_nodes, width)

    back = lax.map(source_block, jnp.arange(n_col, dtype=jnp.int32))
    back = jnp.transpose(back, (1, 0, 2, 3)).reshape(-1, width)
    own = lax.dot_general(grad_pre, w_self, (((1,), (1,)), ((), ())), preferred_element_type=jnp.float32)
    grad_features = (own + back).astype(jnp.bfloat16)
    return output, grad_features
```

```python
import functools

import jax
import jax.numpy as jnp
from jax import lax
from jax.experimental import pallas as pl
from jax.experimental.pallas import tpu as pltpu
from jax.sharding import PartitionSpec as P

NY, NZH, NCORE, NX, NZL = 4, 4, 2, 4, 2
NCOL = NX * NZL
TILE = 128
SPLIT_AG = 80
SPLIT_RS = 352
BF16 = jnp.bfloat16
F32 = jnp.float32
MB = 1024 * 1024


def pairs_to(dy=0, dzh=0, dc=0, dx=0, dzl=0):
    out = []
    for y in range(NY):
        for zh in range(NZH):
            for c in range(NCORE):
                for x in range(NX):
                    for zl in range(NZL):
                        src = (((y * NZH + zh) * NCORE + c) * NX + x) * NZL + zl
                        y2, zh2, c2 = (y + dy) % NY, (zh + dzh) % NZH, (c + dc) % NCORE
                        x2, zl2 = (x + dx) % NX, (zl + dzl) % NZL
                        out.append((src, (((y2 * NZH + zh2) * NCORE + c2) * NX + x2) * NZL + zl2))
    return out


def push(value, **ahead):
    return lax.ppermute(value, ("row", "col"), pairs_to(**ahead))


def pull(value, **ahead):
    return push(value, **{k: -v for k, v in ahead.items()})


def adjacency_kernel(order, where, *refs):
    del order
    masks, out = refs[:-1], refs[-1]
    step = pl.program_id(0)
    out[...] = jnp.zeros_like(out)
    slots = masks[0].shape[1]
    for i, mask in enumerate(masks):
        for k in range(slots):
            q = where[(step * len(masks) + i) * slots + k]
            at = pl.ds(pl.multiple_of(q * TILE, TILE), TILE)
            cols = slice(i * TILE, (i + 1) * TILE)
            out[at, cols] = out[at, cols] + mask[0, k].astype(F32).astype(BF16)


def adjacency(masks, order, where):
    count, slots = masks.shape[0], masks.shape[1]
    group = 4
    specs = [
        pl.BlockSpec(
            (1, slots, TILE, TILE),
            functools.partial(lambda i, s, order, where: (order[s * group + i], 0, 0, 0), i),
        )
        for i in range(group)
    ]
    return pl.pallas_call(
        adjacency_kernel,
        grid_spec=pltpu.PrefetchScalarGridSpec(
            num_scalar_prefetch=2,
            grid=(count // group,),
            in_specs=specs,
            out_specs=pl.BlockSpec((NCOL * TILE, group * TILE), lambda s, order, where: (0, s)),
        ),
        out_shape=jax.ShapeDtypeStruct((NCOL * TILE, count * TILE), BF16),
        compiler_params=pltpu.CompilerParams(vmem_limit_bytes=32 * MB),
        cost_estimate=pl.CostEstimate(flops=0, bytes_accessed=14 * MB, transcendentals=0),
        name="adjacency",
    )(order, where, *([masks] * group))


def gather_matmul_kernel(adj, *refs):
    nz = NCORE * NY
    zparts, yparts = refs[:nz], refs[nz : nz + NCORE * NZH]
    own_ref, out_refs = refs[nz + NCORE * NZH], refs[nz + NCORE * NZH + 1 : -2]
    whole, acc = refs[-2:]
    step = pl.program_id(0)
    a, b = SPLIT_AG, TILE - SPLIT_AG

    @pl.when(step == 0)
    def _():
        for c in range(NCORE):
            for dy in range(NY):
                for dzh in range(NZH):
                    at = ((c * NY + dy) * NZH + dzh) * TILE
                    whole[at : at + a, :] = zparts[c * NY + dy][dzh * a : (dzh + 1) * a, :]
                    whole[at + a : at + TILE, :] = yparts[c * NZH + dzh][dy * b : (dy + 1) * b, :]
        acc[...] = jnp.zeros_like(acc)

    depth = NZH * TILE
    rhs = whole[pl.ds(pl.multiple_of(step * depth, depth), depth), :]
    acc[...] += jnp.dot(adj[...], rhs, preferred_element_type=F32)

    @pl.when(step == pl.num_programs(0) - 1)
    def _():
        own_ref[...] = acc[0:TILE, :].astype(BF16)
        for i, out in enumerate(out_refs):
            out[...] = acc[(i + 1) * TILE : (i + 2) * TILE, :].astype(BF16)


def gather_matmul(adj, zparts, yparts):
    width = zparts[0].shape[1]
    rows, cols = adj.shape
    full = lambda v: pl.BlockSpec(v.shape, lambda s: (0,) * v.ndim)
    piece = jax.ShapeDtypeStruct((TILE, width), BF16)
    return pl.pallas_call(
        gather_matmul_kernel,
        grid=(NCORE * NY,),
        in_specs=[pl.BlockSpec((rows, NZH * TILE), lambda s: (0, s))] + [full(v) for v in (*zparts, *yparts)],
        out_specs=[full(piece)] * NCOL,
        out_shape=[piece] * NCOL,
        scratch_shapes=[pltpu.VMEM((cols, width), BF16), pltpu.VMEM((rows, width), F32)],
        compiler_params=pltpu.CompilerParams(vmem_limit_bytes=48 * MB),
        cost_estimate=pl.CostEstimate(flops=2 * rows * cols * width, bytes_accessed=14 * MB, transcendentals=0),
        name="gather_matmul",
    )(adj, *zparts, *yparts)


def node_kernel(*refs):
    parts = refs[:NCOL]
    base, degf_col, degf_row, w_neigh, cotangent, out, grad, scaled_t = refs[NCOL:]
    total = parts[0][...].astype(F32)
    for part in parts[1:]:
        total = total + part[...].astype(F32)
    mean = (total / degf_col[...]).astype(BF16)
    pre = base[...] + jnp.dot(mean, w_neigh[...], preferred_element_type=F32)
    sig = jax.nn.sigmoid(pre)
    out[...] = (pre * sig).astype(BF16)
    slope = sig * (1.0 + pre * (1.0 - sig))
    grad_pre = (cotangent[...].astype(F32) * slope).astype(BF16)
    grad[...] = grad_pre
    proj_t = lax.dot_general(w_neigh[...], grad_pre, (((1,), (1,)), ((), ())), preferred_element_type=F32)
    scaled_t[...] = (proj_t / degf_row[...]).astype(BF16)


def node_step(parts, base, degf, w_neigh, cotangent):
    rows, width = cotangent.shape
    return pl.pallas_call(
        node_kernel,
        out_shape=[
            jax.ShapeDtypeStruct((rows, width), BF16),
            jax.ShapeDtypeStruct((rows, width), BF16),
            jax.ShapeDtypeStruct((width, rows), BF16),
        ],
        compiler_params=pltpu.CompilerParams(vmem_limit_bytes=32 * MB),
        cost_estimate=pl.CostEstimate(flops=4 * rows * width * width, bytes_accessed=3 * MB, transcendentals=rows * width),
        name="node_step",
    )(*parts, base, degf[:, None], degf[None, :], w_neigh, cotangent)


def spread_matmul_kernel(*refs):
    parts, adj, out = refs[:NCOL], refs[NCOL], refs[NCOL + 1]
    lhs = jnp.concatenate([part[...] for part in parts], axis=1)
    out[...] = jnp.dot(lhs, adj[...], preferred_element_type=F32).astype(BF16)


def spread_matmul(parts, adj, half):
    width = parts[0].shape[0]
    rows = adj.shape[0]
    steps = NY
    full = lambda v: pl.BlockSpec(v.shape, lambda s: (0,) * v.ndim)
    return pl.pallas_call(
        spread_matmul_kernel,
        grid=(steps,),
        in_specs=[full(v) for v in parts] + [pl.BlockSpec((rows, NZH * TILE), lambda s: (0, half * steps + s))],
        out_specs=pl.BlockSpec((width, NZH * TILE), lambda s: (0, s)),
        out_shape=jax.ShapeDtypeStruct((width, steps * NZH * TILE), BF16),
        compiler_params=pltpu.CompilerParams(vmem_limit_bytes=32 * MB),
        cost_estimate=pl.CostEstimate(flops=2 * rows * width * steps * NZH * TILE, bytes_accessed=7 * MB, transcendentals=0),
        name="spread_matmul",
    )(*parts, adj)


def pair_kernel(mine, theirs, *outs):
    total = (mine[...].astype(F32) + theirs[...].astype(F32)).astype(BF16)
    zouts, youts = outs[:NY], outs[NY:]
    for dy in range(NY):
        zouts[dy][...] = total[:SPLIT_RS, dy * NZH * TILE : (dy + 1) * NZH * TILE]
    for dzh in range(NZH):
        for dy in range(NY):
            at = (dy * NZH + dzh) * TILE
            youts[dzh][:, dy * TILE : (dy + 1) * TILE] = total[SPLIT_RS:, at : at + TILE]


def pair_sum(mine, theirs):
    width = mine.shape[0]
    return pl.pallas_call(
        pair_kernel,
        out_shape=[jax.ShapeDtypeStruct((SPLIT_RS, NZH * TILE), BF16)] * NY
        + [jax.ShapeDtypeStruct((width - SPLIT_RS, NY * TILE), BF16)] * NZH,
        compiler_params=pltpu.CompilerParams(vmem_limit_bytes=32 * MB),
        cost_estimate=pl.CostEstimate(flops=width * 2048, bytes_accessed=6 * MB, transcendentals=0),
        name="pair_sum",
    )(mine, theirs)


def add_kernel(*refs):
    total = refs[0][...].astype(F32)
    for ref in refs[1:-4]:
        total = total + ref[...].astype(F32)
    total = total.astype(BF16)
    for i, out in enumerate(refs[-4:]):
        out[...] = total[:, i * TILE : (i + 1) * TILE]


def add_split(values, name):
    rows = values[0].shape[0]
    return pl.pallas_call(
        add_kernel,
        out_shape=[jax.ShapeDtypeStruct((rows, TILE), BF16)] * 4,
        compiler_params=pltpu.CompilerParams(vmem_limit_bytes=32 * MB),
        cost_estimate=pl.CostEstimate(flops=rows * 2048, bytes_accessed=2 * MB, transcendentals=0),
        name=name,
    )(*values)


def last_kernel(*refs):
    zvals, yvals, own, out = refs[:NZH], refs[NZH : NZH + NY], refs[-2], refs[-1]
    upper = zvals[0][...].astype(F32)
    for ref in zvals[1:]:
        upper = upper + ref[...].astype(F32)
    lower = yvals[0][...].astype(F32)
    for ref in yvals[1:]:
        lower = lower + ref[...].astype(F32)
    back = jnp.concatenate([upper, lower], axis=0)
    out[...] = (own[...] + back.T).astype(BF16)


def last_sum(zvals, yvals, own):
    return pl.pallas_call(
        last_kernel,
        out_shape=jax.ShapeDtypeStruct(own.shape, BF16),
        compiler_params=pltpu.CompilerParams(vmem_limit_bytes=32 * MB),
        name="last_sum",
    )(*zvals, *yvals, own)


def body(features, degrees, tile_rows, tile_masks, w_self, w_neigh, bias, cotangent):
    row, col = lax.axis_index("row"), lax.axis_index("col")
    y, zh, core = row // (NZH * NCORE), (row // NCORE) % NZH, row % NCORE
    x, zl = col // NZL, col % NZL

    m = jnp.arange(NCORE * NY * NZH, dtype=jnp.int32)
    order = (((y + m // NZH) % NY) * NZH + (zh + m) % NZH) * NCORE + (core + m // (NY * NZH)) % NCORE
    order = order.astype(jnp.int32)
    rows_here = tile_rows[0, 0]
    rel = ((rows_here // NZL - x) % NX) * NZL + (rows_here - zl) % NZL
    where = rel[order].reshape(-1).astype(jnp.int32)

    top, rest = features[:SPLIT_AG], features[SPLIT_AG:]
    ztop = [top] + [pull(top, dzh=d) for d in (1, 3, 2)]
    ztop = jnp.concatenate([ztop[0], ztop[1], ztop[3], ztop[2]], axis=0)
    yrest = [rest] + [pull(rest, dy=d) for d in (1, 3, 2)]
    yrest = jnp.concatenate([yrest[0], yrest[1], yrest[3], yrest[2]], axis=0)
    zparts = [ztop] + [pull(ztop, dy=d) for d in (1, 2, 3)]
    yparts = [yrest] + [pull(yrest, dzh=d) for d in (1, 2, 3)]
    zparts = zparts + [push(v, dc=1) for v in zparts]
    yparts = yparts + [push(v, dc=1) for v in yparts]

    adj = adjacency(tile_masks[0, 0], order, where)
    parts = gather_matmul(adj, zparts, yparts)

    arrived = [parts[0]]
    for i in range(1, NCOL):
        arrived.append(push(parts[i], dx=i // NZL, dzl=i % NZL))
    degf = degrees.astype(F32)
    base = jnp.dot(features, w_self, preferred_element_type=F32) + bias[None, :]
    output, grad_pre, scaled_t = node_step(arrived, base, degf, w_neigh, cotangent)

    table = [scaled_t] + [pull(scaled_t, dx=i // NZL, dzl=i % NZL) for i in range(1, NCOL)]
    own = lax.dot_general(grad_pre, w_self, (((1,), (1,)), ((), ())), preferred_element_type=F32)
    theirs = push(spread_matmul(table, adj, 1), dc=1)
    mine = spread_matmul(table, adj, 0)
    sums = pair_sum(mine, theirs)
    zsums, ysums = sums[:NY], sums[NY:]
    zgot = [zsums[0]] + [push(zsums[d], dy=d) for d in (1, 3, 2)]
    ygot = [ysums[0]] + [push(ysums[d], dzh=d) for d in (1, 3, 2)]
    zlast = add_split(zgot, "add_z")
    ylast = add_split(ygot, "add_y")
    zend = [zlast[0]] + [push(zlast[d], dzh=d) for d in (1, 3, 2)]
    yend = [ylast[0]] + [push(ylast[d], dy=d) for d in (1, 3, 2)]
    grad_features = last_sum(zend, yend, own)
    return output, grad_features


def solution(mesh):
    both = P(("row", "col"), None)
    return jax.shard_map(
        body,
        mesh=mesh,
        in_specs=(
            both,
            P(("row", "col")),
            P("row", "col", None, None),
            P("row", "col", None, None, None, None),
            P(),
            P(),
            P(),
            both,
        ),
        out_specs=(both, both),
        check_vma=False,
    )
```

```python
import functools

import jax
import jax.numpy as jnp
from jax import lax
from jax.experimental import pallas as pl
from jax.experimental.pallas import tpu as pltpu
from jax.sharding import PartitionSpec as P

NY, NZH, NCORE, NX, NZL = 4, 4, 2, 4, 2
NROW, NCOL = NY * NZH * NCORE, NX * NZL
CHIPS = NY * NZH
TILE = 128
BF16 = jnp.bfloat16
F32 = jnp.float32
MB = 1024 * 1024


def device(y, zh, c, col):
    return ((y * NZH + zh) * NCORE + c) * NCOL + col


def groups_along(axis):
    out = []
    for c in range(NCORE):
        if axis == "y":
            for zh in range(NZH):
                out.append([(y * NZH + zh) * NCORE + c for y in range(NY)])
        else:
            for y in range(NY):
                out.append([(y * NZH + zh) * NCORE + c for zh in range(NZH)])
    return out


def exchange(value, axis):
    return lax.all_to_all(value, "row", 0, 0, axis_index_groups=groups_along(axis), tiled=True)


def swap(value):
    pairs = [
        (device(y, zh, c, col), device(y, zh, 1 - c, col))
        for y in range(NY)
        for zh in range(NZH)
        for c in range(NCORE)
        for col in range(NCOL)
    ]
    return lax.ppermute(value, ("row", "col"), pairs)


def adjacency_kernel(order, where, *refs):
    masks, out = refs[:-1], refs[-1]
    step = pl.program_id(0)
    out[...] = jnp.zeros_like(out)
    slots = masks[0].shape[1]
    for i, mask in enumerate(masks):
        j = order[step * len(masks) + i]
        for k in range(slots):
            q = where[j * slots + k]
            at = pl.ds(pl.multiple_of(q * TILE, TILE), TILE)
            cols = slice(i * TILE, (i + 1) * TILE)
            out[at, cols] = out[at, cols] + mask[0, k].astype(F32).astype(BF16)


def adjacency(masks, order, where):
    count, slots = masks.shape[0], masks.shape[1]
    group = 4
    specs = [
        pl.BlockSpec(
            (1, slots, TILE, TILE),
            functools.partial(lambda i, s, order, where: (order[s * group + i], 0, 0, 0), i),
        )
        for i in range(group)
    ]
    return pl.pallas_call(
        adjacency_kernel,
        grid_spec=pltpu.PrefetchScalarGridSpec(
            num_scalar_prefetch=2,
            grid=(count // group,),
            in_specs=specs,
            out_specs=pl.BlockSpec((NCOL * TILE, group * TILE), lambda s, order, where: (0, s)),
        ),
        out_shape=jax.ShapeDtypeStruct((NCOL * TILE, count * TILE), BF16),
        compiler_params=pltpu.CompilerParams(vmem_limit_bytes=32 * MB),
        cost_estimate=pl.CostEstimate(flops=0, bytes_accessed=14 * MB, transcendentals=0),
        name="adjacency",
    )(order, where, *([masks] * group))


def first_half_kernel(adj, x, out):
    @pl.when(pl.program_id(0) == 0)
    def _():
        out[...] = jnp.zeros_like(out)

    out[...] += jnp.dot(adj[...], x[...], preferred_element_type=F32)


def first_half(adj, x):
    rows, width = adj.shape[0], x.shape[1]
    depth = NZH * TILE
    return pl.pallas_call(
        first_half_kernel,
        grid=(x.shape[0] // depth,),
        in_specs=[
            pl.BlockSpec((rows, depth), lambda s: (0, s)),
            pl.BlockSpec((depth, width), lambda s: (s, 0)),
        ],
        out_specs=pl.BlockSpec((rows, width), lambda s: (0, 0)),
        out_shape=jax.ShapeDtypeStruct((rows, width), F32),
        compiler_params=pltpu.CompilerParams(vmem_limit_bytes=32 * MB),
        cost_estimate=pl.CostEstimate(flops=2 * rows * x.shape[0] * width, bytes_accessed=8 * MB, transcendentals=0),
        name="first_half",
    )(adj, x)


def second_half_kernel(adj, x, start, out, acc):
    @pl.when(pl.program_id(0) == 0)
    def _():
        acc[...] = start[...]

    acc[...] += jnp.dot(adj[...], x[...], preferred_element_type=F32)

    @pl.when(pl.program_id(0) == pl.num_programs(0) - 1)
    def _():
        out[...] = acc[...].astype(BF16)


def second_half(adj, x, start):
    rows, width = adj.shape[0], x.shape[1]
    depth = NZH * TILE
    return pl.pallas_call(
        second_half_kernel,
        grid=(x.shape[0] // depth,),
        in_specs=[
            pl.BlockSpec((rows, depth), lambda s: (0, NY + s)),
            pl.BlockSpec((depth, width), lambda s: (s, 0)),
            pl.BlockSpec((rows, width), lambda s: (0, 0)),
        ],
        out_specs=pl.BlockSpec((rows, width), lambda s: (0, 0)),
        out_shape=jax.ShapeDtypeStruct((rows, width), BF16),
        scratch_shapes=[pltpu.VMEM((rows, width), F32)],
        compiler_params=pltpu.CompilerParams(vmem_limit_bytes=32 * MB),
        cost_estimate=pl.CostEstimate(flops=2 * rows * x.shape[0] * width, bytes_accessed=9 * MB, transcendentals=0),
        name="second_half",
    )(adj, x, start)


def node_kernel(parts, base, degf_col, degf_row, w_neigh, cotangent, out, grad, scaled_t):
    total = parts[0:TILE, :].astype(F32)
    for i in range(1, NCOL):
        total = total + parts[i * TILE : (i + 1) * TILE, :].astype(F32)
    mean = (total / degf_col[...]).astype(BF16)
    pre = base[...] + jnp.dot(mean, w_neigh[...], preferred_element_type=F32)
    sig = jax.nn.sigmoid(pre)
    out[...] = (pre * sig).astype(BF16)
    slope = sig * (1.0 + pre * (1.0 - sig))
    grad_pre = (cotangent[...].astype(F32) * slope).astype(BF16)
    grad[...] = grad_pre
    proj_t = lax.dot_general(w_neigh[...], grad_pre, (((1,), (1,)), ((), ())), preferred_element_type=F32)
    scaled = (proj_t / degf_row[...]).astype(BF16)
    for i in range(NCOL):
        scaled_t[i, :, :] = scaled


def node_step(parts, base, degf, w_neigh, cotangent):
    rows, width = cotangent.shape
    return pl.pallas_call(
        node_kernel,
        out_shape=[
            jax.ShapeDtypeStruct((rows, width), BF16),
            jax.ShapeDtypeStruct((rows, width), BF16),
            jax.ShapeDtypeStruct((NCOL, width, rows), BF16),
        ],
        compiler_params=pltpu.CompilerParams(vmem_limit_bytes=32 * MB),
        cost_estimate=pl.CostEstimate(flops=4 * rows * width * width, bytes_accessed=4 * MB, transcendentals=rows * width),
        name="node_step",
    )(parts, base, degf[:, None], degf[None, :], w_neigh, cotangent)


def spread_matmul_kernel(parts, adj, out):
    lhs = jnp.concatenate([parts[i] for i in range(NCOL)], axis=1)
    out[0] = jnp.dot(lhs, adj[...], preferred_element_type=F32).astype(BF16)


def spread_matmul(parts, adj, half):
    width = parts.shape[1]
    rows = adj.shape[0]
    return pl.pallas_call(
        spread_matmul_kernel,
        grid=(NY,),
        in_specs=[
            pl.BlockSpec(parts.shape, lambda s: (0, 0, 0)),
            pl.BlockSpec((rows, NZH * TILE), lambda s: (0, half * NY + s)),
        ],
        out_specs=pl.BlockSpec((1, width, NZH * TILE), lambda s: (s, 0, 0)),
        out_shape=jax.ShapeDtypeStruct((NY, width, NZH * TILE), BF16),
        compiler_params=pltpu.CompilerParams(vmem_limit_bytes=32 * MB),
        cost_estimate=pl.CostEstimate(flops=2 * rows * width * CHIPS * TILE, bytes_accessed=7 * MB, transcendentals=0),
        name="spread_matmul",
    )(parts, adj)


def pair_kernel(mine, theirs, out):
    out[...] = (mine[...].astype(F32) + theirs[...].astype(F32)).astype(BF16)


def pair_sum(mine, theirs):
    spec = pl.BlockSpec((1, *mine.shape[1:]), lambda s: (s, 0, 0))
    return pl.pallas_call(
        pair_kernel,
        grid=(mine.shape[0],),
        in_specs=[spec, spec],
        out_specs=spec,
        out_shape=jax.ShapeDtypeStruct(mine.shape, BF16),
        compiler_params=pltpu.CompilerParams(vmem_limit_bytes=32 * MB),
        cost_estimate=pl.CostEstimate(flops=MB, bytes_accessed=6 * MB, transcendentals=0),
        name="pair_sum",
    )(mine, theirs)


def add_kernel(parts, out):
    total = parts[0].astype(F32)
    for i in range(1, parts.shape[0]):
        total = total + parts[i].astype(F32)
    total = total.astype(BF16)
    for i in range(NZH):
        out[i, :, :] = total[:, i * TILE : (i + 1) * TILE]


def add_split(parts):
    width = parts.shape[1]
    return pl.pallas_call(
        add_kernel,
        out_shape=jax.ShapeDtypeStruct((NZH, width, TILE), BF16),
        compiler_params=pltpu.CompilerParams(vmem_limit_bytes=32 * MB),
        cost_estimate=pl.CostEstimate(flops=MB, bytes_accessed=3 * MB, transcendentals=0),
        name="add_split",
    )(parts)


def last_kernel(parts, own, out):
    back = parts[0].astype(F32)
    for i in range(1, parts.shape[0]):
        back = back + parts[i].astype(F32)
    out[...] = (own[...] + back.T).astype(BF16)


def last_sum(parts, own):
    return pl.pallas_call(
        last_kernel,
        out_shape=jax.ShapeDtypeStruct(own.shape, BF16),
        compiler_params=pltpu.CompilerParams(vmem_limit_bytes=32 * MB),
        name="last_sum",
    )(parts, own)


def repeat(value, times):
    return jnp.broadcast_to(value[None], (times, *value.shape))


def body(features, degrees, tile_rows, tile_masks, w_self, w_neigh, bias, cotangent):
    width = features.shape[1]
    core = lax.axis_index("row") % NCORE

    m = jnp.arange(NROW, dtype=jnp.int32)
    order = (m % CHIPS) * NCORE + jnp.where(m < CHIPS, core, 1 - core).astype(jnp.int32)
    adj = adjacency(tile_masks[0, 0], order, tile_rows[0, 0].reshape(-1))

    near = exchange(repeat(features, NZH), "z").reshape(NZH * TILE, width)
    mine = exchange(repeat(near, NY), "y").reshape(CHIPS * TILE, width)
    theirs = swap(mine)
    summed = second_half(adj, theirs, first_half(adj, mine))

    arrived = lax.all_to_all(summed, "col", 0, 0, tiled=True)
    degf = degrees.astype(F32)
    base = jnp.dot(features, w_self, preferred_element_type=F32) + bias[None, :]
    output, grad_pre, scaled_t = node_step(arrived, base, degf, w_neigh, cotangent)

    table = lax.all_to_all(scaled_t, "col", 0, 0, tiled=True)
    own = lax.dot_general(grad_pre, w_self, (((1,), (1,)), ((), ())), preferred_element_type=F32)
    theirs = swap(spread_matmul(table, adj, 1))
    mine = spread_matmul(table, adj, 0)
    sums = add_split(exchange(pair_sum(mine, theirs), "y"))
    grad_features = last_sum(exchange(sums, "z"), own)
    return output, grad_features


def solution(mesh):
    both = P(("row", "col"), None)
    return jax.shard_map(
        body,
        mesh=mesh,
        in_specs=(
            both,
            P(("row", "col")),
            P("row", "col", None, None),
            P("row", "col", None, None, None, None),
            P(),
            P(),
            P(),
            both,
        ),
        out_specs=(both, both),
        check_vma=False,
    )
```

```python
import functools

import jax
import jax.numpy as jnp
from jax import lax
from jax.experimental import pallas as pl
from jax.experimental.pallas import tpu as pltpu
from jax.sharding import PartitionSpec as P

NY, NZH, NCORE, NX, NZL = 4, 4, 2, 4, 2
NROW, NCOL = NY * NZH * NCORE, NX * NZL
CHIPS = NY * NZH
STEPS = ((1, 3), (3, 1))
TILE = 128
BF16 = jnp.bfloat16
F32 = jnp.float32
MB = 1024 * 1024


def flip(value, y=0, z=0, core=0):
    pairs = []
    for row in range(NROW):
        there = row ^ ((y * NZH + z) * NCORE + core)
        pairs += [(row * NCOL + col, there * NCOL + col) for col in range(NCOL)]
    return lax.ppermute(value, ("row", "col"), pairs)


def adjacency_kernel(order, where, *refs):
    masks, out = refs[:-1], refs[-1]
    step = pl.program_id(0)
    out[...] = jnp.zeros_like(out)
    slots = masks[0].shape[1]
    for i, mask in enumerate(masks):
        j = order[step * len(masks) + i]
        for k in range(slots):
            q = where[j * slots + k]
            at = pl.ds(pl.multiple_of(q * TILE, TILE), TILE)
            cols = slice(i * TILE, (i + 1) * TILE)
            out[at, cols] = out[at, cols] + mask[0, k].astype(F32).astype(BF16)


def adjacency(masks, order, where):
    count, slots = masks.shape[0], masks.shape[1]
    group = 4
    specs = [
        pl.BlockSpec(
            (1, slots, TILE, TILE),
            functools.partial(lambda i, s, order, where: (order[s * group + i], 0, 0, 0), i),
        )
        for i in range(group)
    ]
    masks = pltpu.with_memory_space_constraint(masks, pltpu.HBM)
    return pl.pallas_call(
        adjacency_kernel,
        grid_spec=pltpu.PrefetchScalarGridSpec(
            num_scalar_prefetch=2,
            grid=(count // group,),
            in_specs=specs,
            out_specs=pl.BlockSpec((NCOL * TILE, group * TILE), lambda s, order, where: (0, s)),
        ),
        out_shape=pltpu.HBM((NCOL * TILE, count * TILE), BF16),
        compiler_params=pltpu.CompilerParams(vmem_limit_bytes=16 * MB),
        cost_estimate=pl.CostEstimate(flops=0, bytes_accessed=14 * MB, transcendentals=0),
        name="adjacency",
    )(order, where, *([masks] * group))


def gather_kernel(plan, blocks, adj, *refs):
    del blocks
    parts, refs = refs[:4], refs[4:]
    start, out, acc = (refs[0], refs[1], refs[2]) if len(refs) == 3 else (None, refs[0], refs[0])
    half = parts[0].shape[1]
    depth = NZH * TILE

    @pl.when(pl.program_id(0) == 0)
    def _():
        acc[...] = jnp.zeros_like(acc) if start is None else start[...]

    for step, (_, places) in enumerate(plan):

        @pl.when(pl.program_id(0) == step)
        def _(places=places):
            for h, array, at in places:
                cols = slice(h * half, (h + 1) * half)
                rhs = parts[array][at * depth : (at + 1) * depth, :]
                acc[:, cols] += jnp.dot(adj[...], rhs, preferred_element_type=F32)

    if start is not None:

        @pl.when(pl.program_id(0) == pl.num_programs(0) - 1)
        def _():
            out[...] = acc[...].astype(BF16)


def gather_matmul(adj, parts, dys, start, name):
    plan = []
    for core in range(NCORE):
        for dy in range(NY):
            places = [(h, core * 2 + h, dys[h].index(dy)) for h in range(2) if dy in dys[h]]
            if places:
                plan.append((core * NY + dy, places))
    rows, width = adj.shape[0], 2 * parts[0].shape[1]
    full = lambda shape: pl.BlockSpec(shape, lambda s, blocks: (0, 0))
    specs = [pl.BlockSpec((rows, NZH * TILE), lambda s, blocks: (0, blocks[s]))] + [full(v.shape) for v in parts]
    operands = [pltpu.with_memory_space_constraint(adj, pltpu.HBM), *parts]
    if start is not None:
        specs.append(full((rows, width)))
        operands.append(start)
    return pl.pallas_call(
        functools.partial(gather_kernel, plan),
        grid_spec=pltpu.PrefetchScalarGridSpec(
            num_scalar_prefetch=1,
            grid=(len(plan),),
            in_specs=specs,
            out_specs=full((rows, width)),
            scratch_shapes=[] if start is None else [pltpu.VMEM((rows, width), F32)],
        ),
        out_shape=jax.ShapeDtypeStruct((rows, width), F32) if start is None else pltpu.HBM((rows, width), BF16),
        compiler_params=pltpu.CompilerParams(vmem_limit_bytes=24 * MB),
        cost_estimate=pl.CostEstimate(flops=2 * rows * width * CHIPS * TILE, bytes_accessed=9 * MB, transcendentals=0),
        name=name,
    )(jnp.array([block for block, _ in plan], jnp.int32), *operands)


def node_kernel(parts, base, degf_col, degf_row, w_neigh, cotangent, out, grad, scaled_t):
    total = parts[0:TILE, :].astype(F32)
    for i in range(1, NCOL):
        total = total + parts[i * TILE : (i + 1) * TILE, :].astype(F32)
    mean = (total / degf_col[...]).astype(BF16)
    pre = base[...] + jnp.dot(mean, w_neigh[...], preferred_element_type=F32)
    sig = jax.nn.sigmoid(pre)
    out[...] = (pre * sig).astype(BF16)
    slope = sig * (1.0 + pre * (1.0 - sig))
    grad_pre = (cotangent[...].astype(F32) * slope).astype(BF16)
    grad[...] = grad_pre
    proj_t = lax.dot_general(w_neigh[...], grad_pre, (((1,), (1,)), ((), ())), preferred_element_type=F32)
    scaled = (proj_t / degf_row[...]).astype(BF16)
    for i in range(NCOL):
        scaled_t[i, :, :] = scaled


def node_step(parts, base, degf, w_neigh, cotangent):
    rows, width = cotangent.shape
    return pl.pallas_call(
        node_kernel,
        out_shape=[
            jax.ShapeDtypeStruct((rows, width), BF16),
            jax.ShapeDtypeStruct((rows, width), BF16),
            jax.ShapeDtypeStruct((NCOL, width, rows), BF16),
        ],
        compiler_params=pltpu.CompilerParams(vmem_limit_bytes=32 * MB),
        cost_estimate=pl.CostEstimate(flops=4 * rows * width * width, bytes_accessed=4 * MB, transcendentals=rows * width),
        name="node_step",
    )(parts, base, degf[:, None], degf[None, :], w_neigh, cotangent)


def spread_kernel(parts, adj, keep, send):
    lhs = jnp.concatenate([parts[i] for i in range(NCOL)], axis=1)
    value = jnp.dot(lhs, adj[...], preferred_element_type=F32).astype(BF16)
    half = value.shape[0] // 2
    depth = NZH * TILE
    for dy in range(NY):

        @pl.when(pl.program_id(0) == dy)
        def _(dy=dy):
            for h, (k1, k2) in enumerate(STEPS):
                out, order = (keep, (0, k1)) if dy in (0, k1) else (send, (k2, k1 ^ k2))
                at = order.index(dy) * depth
                out[h, :, at : at + depth] = value[h * half : (h + 1) * half, :]


def spread_matmul(parts, adj, core, name):
    width = parts.shape[1]
    rows = adj.shape[0]
    shape = (2, width // 2, 2 * NZH * TILE)
    return pl.pallas_call(
        spread_kernel,
        grid=(NY,),
        in_specs=[
            pl.BlockSpec(parts.shape, lambda s: (0, 0, 0)),
            pl.BlockSpec((rows, NZH * TILE), lambda s: (0, core * NY + s)),
        ],
        out_specs=[pl.BlockSpec(shape, lambda s: (0, 0, 0))] * 2,
        out_shape=[jax.ShapeDtypeStruct(shape, BF16)] * 2,
        compiler_params=pltpu.CompilerParams(vmem_limit_bytes=24 * MB),
        cost_estimate=pl.CostEstimate(flops=2 * rows * width * CHIPS * TILE, bytes_accessed=7 * MB, transcendentals=0),
        name=name,
    )(parts, pltpu.with_memory_space_constraint(adj, pltpu.HBM))


def total(refs):
    value = refs[0][...].astype(F32)
    for ref in refs[1:]:
        value = value + ref[...].astype(F32)
    return value


def both_halves_kernel(mine, theirs, *outs):
    for h, out in enumerate(outs):
        out[...] = (mine[h].astype(F32) + theirs[h].astype(F32)).astype(BF16)


def both_halves(mine, theirs):
    shape = mine.shape[1:]
    return pl.pallas_call(
        both_halves_kernel,
        out_shape=[jax.ShapeDtypeStruct(shape, BF16)] * 2,
        compiler_params=pltpu.CompilerParams(vmem_limit_bytes=16 * MB),
        cost_estimate=pl.CostEstimate(flops=MB, bytes_accessed=3 * MB, transcendentals=0),
        name="both_halves",
    )(mine, theirs)


def split_kernel(kept, sent, *refs):
    value = total(refs[:-2])
    for out, tiles in zip(refs[-2:], (kept, sent)):
        for i, tile in enumerate(tiles):
            part = value[:, tile * TILE : (tile + 1) * TILE]
            out[:, i * TILE : (i + 1) * TILE] = part.astype(out.dtype)


def add_split(values, kept, sent, name):
    rows = values[0].shape[0]
    return pl.pallas_call(
        functools.partial(split_kernel, kept, sent),
        out_shape=[
            jax.ShapeDtypeStruct((rows, len(kept) * TILE), F32),
            jax.ShapeDtypeStruct((rows, len(sent) * TILE), BF16),
        ],
        compiler_params=pltpu.CompilerParams(vmem_limit_bytes=16 * MB),
        cost_estimate=pl.CostEstimate(flops=MB, bytes_accessed=2 * MB, transcendentals=0),
        name=name,
    )(*values)


def last_kernel(*refs):
    own, out = refs[-2:]
    back = jnp.concatenate([total(refs[0:2]), total(refs[2:4])], axis=0)
    out[...] = (own[...] + back.T).astype(BF16)


def last_sum(values, own):
    return pl.pallas_call(
        last_kernel,
        out_shape=jax.ShapeDtypeStruct(own.shape, BF16),
        compiler_params=pltpu.CompilerParams(vmem_limit_bytes=16 * MB),
        name="last_sum",
    )(*values, own)


def body(features, degrees, tile_rows, tile_masks, w_self, w_neigh, bias, cotangent):
    half = features.shape[1] // 2
    row = lax.axis_index("row").astype(jnp.int32)

    m = jnp.arange(NROW, dtype=jnp.int32)
    order = row ^ ((m % CHIPS) * NCORE + m // CHIPS)
    adj = adjacency(tile_masks[0, 0], order, tile_rows[0, 0].reshape(-1))

    chunks = [features[:, :half], features[:, half:]]
    firsts = [flip(v, z=k1) for v, (k1, _) in zip(chunks, STEPS)]
    pairs = [jnp.concatenate([v, r], axis=0) for v, r in zip(chunks, firsts)]
    seconds = [flip(v, z=k2) for v, (_, k2) in zip(pairs, STEPS)]
    planes = []
    for v, first, second, (k1, k2) in zip(chunks, firsts, seconds, STEPS):
        tiles = {0: v, k1: first, k2: second[:TILE], k1 ^ k2: second[TILE:]}
        planes.append(jnp.concatenate([tiles[i] for i in range(NZH)], axis=0))
    thirds = [flip(v, y=k1) for v, (k1, _) in zip(planes, STEPS)]
    *thirds, adj = lax.optimization_barrier((*thirds, adj))
    near = [jnp.concatenate([v, r], axis=0) for v, r in zip(planes, thirds)]
    far = [flip(v, y=k2) for v, (_, k2) in zip(near, STEPS)]
    near = near + [flip(v, core=1) for v in near]
    start = gather_matmul(adj, near, [(0, k1) for k1, _ in STEPS], None, "gather_near")
    *far, start = lax.optimization_barrier((*far, start))
    far = far + [flip(v, core=1) for v in far]
    summed = gather_matmul(adj, far, [(k2, k1 ^ k2) for k1, k2 in STEPS], start, "gather_far")

    arrived = lax.all_to_all(summed, "col", 0, 0, tiled=True)
    degf = degrees.astype(F32)
    base = jnp.dot(features, w_self, preferred_element_type=F32) + bias[None, :]
    output, grad_pre, scaled_t = node_step(arrived, base, degf, w_neigh, cotangent)

    table = lax.all_to_all(scaled_t, "col", 0, 0, tiled=True)
    own = lax.dot_general(grad_pre, w_self, (((1,), (1,)), ((), ())), preferred_element_type=F32)
    keep_out, send_out = spread_matmul(table, adj, 1, "spread_other")
    send_in, keep_in = flip(send_out, core=1), flip(keep_out, core=1)
    keep, send = spread_matmul(table, adj, 0, "spread_own")

    ends = []
    for h, (value, (k1, k2)) in enumerate(zip(both_halves(send, send_in), STEPS)):
        got = flip(value, y=k2)
        stay, go = add_split((keep[h], keep_in[h], got), range(NZH), range(NZH, 2 * NZH), "add_y1")
        got = flip(go, y=k1)
        stay, go = add_split((stay, got), (0, k1), (k2, k1 ^ k2), "add_y2")
        got = flip(go, z=k2)
        stay, go = add_split((stay, got), (0,), (1,), "add_z1")
        ends += [stay, flip(go, z=k1)]
    grad_features = last_sum(ends, own)
    return output, grad_features


def solution(mesh):
    both = P(("row", "col"), None)
    return jax.shard_map(
        body,
        mesh=mesh,
        in_specs=(
            both,
            P(("row", "col")),
            P("row", "col", None, None),
            P("row", "col", None, None, None, None),
            P(),
            P(),
            P(),
            both,
        ),
        out_specs=(both, both),
        check_vma=False,
    )
```

```python
import functools

import jax
import jax.numpy as jnp
from jax import lax
from jax.experimental import pallas as pl
from jax.experimental.pallas import tpu as pltpu
from jax.sharding import PartitionSpec as P

NY, NZH, NCORE, NX, NZL = 4, 4, 2, 4, 2
NROW, NCOL = NY * NZH * NCORE, NX * NZL
CHIPS = NY * NZH
STEPS = ((1, 3), (3, 1))
TILE = 128
BF16 = jnp.bfloat16
F32 = jnp.float32
MB = 1024 * 1024


def flip(value, y=0, z=0, core=0):
    pairs = []
    for row in range(NROW):
        there = row ^ ((y * NZH + z) * NCORE + core)
        pairs += [(row * NCOL + col, there * NCOL + col) for col in range(NCOL)]
    return lax.ppermute(value, ("row", "col"), pairs)


def in_vmem(kernel, results, operands, name, flops=MB, grant=16, **extra):
    spec = pl.BlockSpec(memory_space=pltpu.VMEM)
    outs = [shape if plain else pltpu.VMEM(shape.shape, shape.dtype) for shape, plain in results]
    out_specs = [pl.BlockSpec() if plain else spec for _, plain in results]
    return pl.pallas_call(
        kernel,
        in_specs=[spec] * len(operands),
        out_specs=out_specs,
        out_shape=outs,
        compiler_params=pltpu.CompilerParams(vmem_limit_bytes=grant * MB),
        cost_estimate=pl.CostEstimate(flops=flops, bytes_accessed=3 * MB, transcendentals=0),
        name=name,
        **extra,
    )(*[pltpu.with_memory_space_constraint(v, pltpu.VMEM) for v in operands])


def kept(shape, dtype):
    return jax.ShapeDtypeStruct(shape, dtype), False


def plain(shape, dtype):
    return jax.ShapeDtypeStruct(shape, dtype), True


def adjacency_kernel(place, where, masks, out, held, sems):
    count, slots = masks.shape[0], masks.shape[1]
    copies = [pltpu.make_async_copy(masks.at[j], held.at[j], sems.at[j]) for j in range(count)]
    for copy in copies:
        copy.start()
    for j, copy in enumerate(copies):
        cols = pl.ds(pl.multiple_of(place[j] * TILE, TILE), TILE)
        out[:, cols] = jnp.zeros((out.shape[0], TILE), BF16)
        copy.wait()
        for k in range(slots):
            at = pl.ds(pl.multiple_of(where[j * slots + k] * TILE, TILE), TILE)
            out[at, cols] = out[at, cols] + held[j, k].astype(F32).astype(BF16)


def adjacency(masks, place, where):
    count = masks.shape[0]
    return pl.pallas_call(
        adjacency_kernel,
        grid_spec=pltpu.PrefetchScalarGridSpec(
            num_scalar_prefetch=2,
            grid=(1,),
            in_specs=[pl.BlockSpec(memory_space=pl.ANY)],
            out_specs=pl.BlockSpec(memory_space=pltpu.VMEM),
            scratch_shapes=[pltpu.VMEM(masks.shape, masks.dtype), pltpu.SemaphoreType.DMA((count,))],
        ),
        out_shape=pltpu.VMEM((NCOL * TILE, count * TILE), BF16),
        compiler_params=pltpu.CompilerParams(vmem_limit_bytes=16 * MB),
        cost_estimate=pl.CostEstimate(flops=0, bytes_accessed=14 * MB, transcendentals=0),
        name="adjacency",
    )(place, where, pltpu.with_memory_space_constraint(masks, pltpu.HBM))


def gather_kernel(cores, dys, adj, *refs):
    parts, out = refs[: 2 * len(cores)], refs[-1]
    start = refs[-2] if len(refs) > len(parts) + 1 else None
    half = parts[0].shape[1]
    depth = NZH * TILE
    rows = 2 * TILE
    for r in range(0, out.shape[0], rows):
        for h in range(2):
            cols = slice(h * half, (h + 1) * half)
            value = None if start is None else start[r : r + rows, cols]
            for i, core in enumerate(cores):
                at = [(core * NY + dy) * depth for dy in dys[h]]
                lhs = jnp.concatenate([adj[r : r + rows, a : a + depth] for a in at], axis=1)
                term = jnp.dot(lhs, parts[2 * i + h][...], preferred_element_type=F32)
                value = term if value is None else value + term
            out[r : r + rows, cols] = value.astype(out.dtype)


def gather_matmul(adj, parts, cores, dys, start, dtype, name):
    rows, width = adj.shape[0], 2 * parts[0].shape[1]
    operands = [adj, *parts] + ([] if start is None else [start])
    flops = 2 * rows * width * parts[0].shape[0] * len(cores)
    return in_vmem(functools.partial(gather_kernel, cores, dys), [kept((rows, width), dtype)], operands, name, flops)[0]


def node_kernel(parts, base, degf_row, w_neigh, cotangent, grad, scaled_t, out):
    total = parts[0:TILE, :].astype(F32)
    for i in range(1, NCOL):
        total = total + parts[i * TILE : (i + 1) * TILE, :].astype(F32)
    degf_col = jnp.broadcast_to(degf_row[...], (TILE, TILE)).T[:, :1]
    mean = (total / degf_col).astype(BF16)
    pre = base[...] + jnp.dot(mean, w_neigh[...], preferred_element_type=F32)
    sig = jax.nn.sigmoid(pre)
    out[...] = (pre * sig).astype(BF16)
    slope = sig * (1.0 + pre * (1.0 - sig))
    grad_pre = (cotangent[...].astype(F32) * slope).astype(BF16)
    grad[...] = grad_pre
    proj_t = lax.dot_general(w_neigh[...], grad_pre, (((1,), (1,)), ((), ())), preferred_element_type=F32)
    scaled = (proj_t / degf_row[...]).astype(BF16)
    for i in range(NCOL):
        scaled_t[i, :, :] = scaled


def node_step(parts, base, degf_row, w_neigh, cotangent):
    rows, width = cotangent.shape
    results = [kept((rows, width), BF16), kept((NCOL, width, rows), BF16), plain((rows, width), BF16)]
    operands = (parts, base, degf_row, w_neigh, cotangent)
    return in_vmem(node_kernel, results, operands, "node_step", 4 * rows * width * width)


def spread_kernel(core, parts, adj, keep, send):
    lhs = jnp.concatenate([parts[i] for i in range(NCOL)], axis=1)
    half = lhs.shape[0] // 2
    depth = NZH * TILE
    for dy in range(NY):
        at = (core * NY + dy) * depth
        value = jnp.dot(lhs, adj[:, at : at + depth], preferred_element_type=F32).astype(BF16)
        for h, (k1, k2) in enumerate(STEPS):
            out, order = (keep, (0, k1)) if dy in (0, k1) else (send, (k2, k1 ^ k2))
            to = order.index(dy) * depth
            out[h, :, to : to + depth] = value[h * half : (h + 1) * half, :]


def spread_matmul(parts, adj, core, name):
    width = parts.shape[1]
    shape = (2, width // 2, 2 * NZH * TILE)
    flops = 2 * adj.shape[0] * width * CHIPS * TILE
    return in_vmem(functools.partial(spread_kernel, core), [kept(shape, BF16)] * 2, (parts, adj), name, flops)


def total(refs):
    value = refs[0][...].astype(F32)
    for ref in refs[1:]:
        value = value + ref[...].astype(F32)
    return value


def both_halves_kernel(mine, theirs, *outs):
    for h, out in enumerate(outs):
        out[...] = (mine[h].astype(F32) + theirs[h].astype(F32)).astype(BF16)


def both_halves(mine, theirs):
    return in_vmem(both_halves_kernel, [kept(mine.shape[1:], BF16)] * 2, (mine, theirs), "both_halves")


def first_split_kernel(h, mine, theirs, got, stay, go):
    value = mine[h].astype(F32) + theirs[h].astype(F32) + got[...].astype(F32)
    depth = stay.shape[1]
    stay[...] = value[:, :depth]
    go[...] = value[:, depth:].astype(BF16)


def first_split(h, mine, theirs, got, name):
    shape = (got.shape[0], got.shape[1] // 2)
    results = [kept(shape, F32), kept(shape, BF16)]
    return in_vmem(functools.partial(first_split_kernel, h), results, (mine, theirs, got), name)


def split_kernel(stays, goes, *refs):
    value = total(refs[:-2])
    for out, tiles in zip(refs[-2:], (stays, goes)):
        for i, tile in enumerate(tiles):
            part = value[:, tile * TILE : (tile + 1) * TILE]
            out[:, i * TILE : (i + 1) * TILE] = part.astype(out.dtype)


def add_split(values, stays, goes, name):
    rows = values[0].shape[0]
    results = [kept((rows, len(stays) * TILE), F32), kept((rows, len(goes) * TILE), BF16)]
    return in_vmem(functools.partial(split_kernel, stays, goes), results, values, name)


def last_kernel(*refs):
    own, out = refs[-2:]
    back = jnp.concatenate([total(refs[0:2]), total(refs[2:4])], axis=0)
    out[...] = (own[...] + back.T).astype(BF16)


def last_sum(values, own):
    return in_vmem(last_kernel, [plain(own.shape, BF16)], (*values, own), "last_sum")[0]


def body(features, degrees, tile_rows, tile_masks, w_self, w_neigh, bias, cotangent):
    half = features.shape[1] // 2
    row = lax.axis_index("row").astype(jnp.int32)

    differ = jnp.arange(NROW, dtype=jnp.int32) ^ row
    adj = adjacency(tile_masks[0, 0], (differ % NCORE) * CHIPS + differ // NCORE, tile_rows[0, 0].reshape(-1))
    degf_row = degrees.astype(F32)[None, :]
    base = jnp.dot(features, w_self, preferred_element_type=F32) + bias[None, :]

    chunks = [features[:, :half], features[:, half:]]
    firsts = [flip(v, z=k1) for v, (k1, _) in zip(chunks, STEPS)]
    pairs = [jnp.concatenate([v, r], axis=0) for v, r in zip(chunks, firsts)]
    seconds = [flip(v, z=k2) for v, (_, k2) in zip(pairs, STEPS)]
    planes = []
    for v, first, second, (k1, k2) in zip(chunks, firsts, seconds, STEPS):
        tiles = {0: v, k1: first, k2: second[:TILE], k1 ^ k2: second[TILE:]}
        planes.append(jnp.concatenate([tiles[i] for i in range(NZH)], axis=0))
    thirds = [flip(v, y=k1) for v, (k1, _) in zip(planes, STEPS)]
    *thirds, adj, base, degf_row = lax.optimization_barrier((*thirds, adj, base, degf_row))
    near = [jnp.concatenate([v, r], axis=0) for v, r in zip(planes, thirds)]
    far = [flip(v, y=k2) for v, (_, k2) in zip(near, STEPS)]
    first, second = [(0, k1) for k1, _ in STEPS], [(k2, k1 ^ k2) for k1, k2 in STEPS]
    near = near + [flip(v, core=1) for v in near]
    part = gather_matmul(adj, near, (0, 1), first, None, F32, "gather_near")
    *far, part = lax.optimization_barrier((*far, part))
    other = [flip(v, core=1) for v in far]
    part = gather_matmul(adj, far, (0,), second, part, F32, "gather_far")
    *other, part = lax.optimization_barrier((*other, part))
    summed = gather_matmul(adj, other, (1,), second, part, BF16, "gather_far_other")

    arrived = lax.all_to_all(summed, "col", 0, 0, tiled=True)
    grad_pre, scaled_t, output = node_step(arrived, base, degf_row, w_neigh, cotangent)

    table = lax.all_to_all(scaled_t, "col", 0, 0, tiled=True)
    own = lax.dot_general(grad_pre, w_self, (((1,), (1,)), ((), ())), preferred_element_type=F32)
    keep_out, send_out = spread_matmul(table, adj, 1, "spread_other")
    send_in, keep_in = flip(send_out, core=1), flip(keep_out, core=1)
    keep, send = spread_matmul(table, adj, 0, "spread_own")

    ends = []
    for h, (value, (k1, k2)) in enumerate(zip(both_halves(send, send_in), STEPS)):
        got = flip(value, y=k2)
        stay, go = first_split(h, keep, keep_in, got, "add_y1")
        got = flip(go, y=k1)
        stay, go = add_split((stay, got), (0, k1), (k2, k1 ^ k2), "add_y2")
        got = flip(go, z=k2)
        stay, go = add_split((stay, got), (0,), (1,), "add_z1")
        ends += [stay, flip(go, z=k1)]
    grad_features = last_sum(ends, own)
    return output, grad_features


def solution(mesh):
    both = P(("row", "col"), None)
    return jax.shard_map(
        body,
        mesh=mesh,
        in_specs=(
            both,
            P(("row", "col")),
            P("row", "col", None, None),
            P("row", "col", None, None, None, None),
            P(),
            P(),
            P(),
            both,
        ),
        out_specs=(both, both),
        check_vma=False,
    )
```

```python
import functools

import jax
import jax.numpy as jnp
from jax import lax
from jax.experimental import pallas as pl
from jax.experimental.pallas import tpu as pltpu
from jax.sharding import PartitionSpec as P

NY, NZH, NCORE, NX, NZL = 4, 4, 2, 4, 2
NROW, NCOL = NY * NZH * NCORE, NX * NZL
CHIPS = NY * NZH
RING = (0, 1, 3, 2)
TILE = 128
BF16 = jnp.bfloat16
F32 = jnp.float32
MB = 1024 * 1024


def flip(value, y=0, z=0, core=0):
    pairs = []
    for row in range(NROW):
        there = row ^ ((y * NZH + z) * NCORE + core)
        pairs += [(row * NCOL + col, there * NCOL + col) for col in range(NCOL)]
    return lax.ppermute(value, ("row", "col"), pairs)


def in_vmem(kernel, results, operands, name, flops=MB, grant=16, **extra):
    spec = pl.BlockSpec(memory_space=pltpu.VMEM)
    outs = [shape if plain else pltpu.VMEM(shape.shape, shape.dtype) for shape, plain in results]
    out_specs = [pl.BlockSpec() if plain else spec for _, plain in results]
    return pl.pallas_call(
        kernel,
        in_specs=[spec] * len(operands),
        out_specs=out_specs,
        out_shape=outs,
        compiler_params=pltpu.CompilerParams(vmem_limit_bytes=grant * MB),
        cost_estimate=pl.CostEstimate(flops=0, bytes_accessed=1024, transcendentals=0),
        name=name,
        **extra,
    )(*[pltpu.with_memory_space_constraint(v, pltpu.VMEM) for v in operands])


def kept(shape, dtype):
    return jax.ShapeDtypeStruct(shape, dtype), False


def plain(shape, dtype):
    return jax.ShapeDtypeStruct(shape, dtype), True


def adjacency_kernel(place, where, masks, out, held, sems):
    count, slots = masks.shape[0], masks.shape[1]
    copies = [pltpu.make_async_copy(masks.at[j], held.at[j], sems.at[j]) for j in range(count)]
    for copy in copies:
        copy.start()
    for j, copy in enumerate(copies):
        cols = pl.ds(pl.multiple_of(place[j] * TILE, TILE), TILE)
        out[:, cols] = jnp.zeros((out.shape[0], TILE), BF16)
        copy.wait()
        for k in range(slots):
            at = pl.ds(pl.multiple_of(where[j * slots + k] * TILE, TILE), TILE)
            out[at, cols] = out[at, cols] + held[j, k].astype(F32).astype(BF16)


def adjacency(masks, place, where):
    count = masks.shape[0]
    return pl.pallas_call(
        adjacency_kernel,
        grid_spec=pltpu.PrefetchScalarGridSpec(
            num_scalar_prefetch=2,
            grid=(1,),
            in_specs=[pl.BlockSpec(memory_space=pl.ANY)],
            out_specs=pl.BlockSpec(memory_space=pltpu.VMEM),
            scratch_shapes=[pltpu.VMEM(masks.shape, masks.dtype), pltpu.SemaphoreType.DMA((count,))],
        ),
        out_shape=pltpu.VMEM((NCOL * TILE, count * TILE), BF16),
        compiler_params=pltpu.CompilerParams(vmem_limit_bytes=16 * MB),
        cost_estimate=pl.CostEstimate(flops=0, bytes_accessed=14 * MB, transcendentals=0),
        name="adjacency",
    )(place, where, pltpu.with_memory_space_constraint(masks, pltpu.HBM))


def gather_kernel(starts, adj, *refs):
    parts, out = refs[: len(starts)], refs[-1]
    start = refs[-2] if len(refs) > len(parts) + 1 else None
    rows = 2 * TILE
    rhs = jnp.concatenate([part[...] for part in parts], axis=0)
    for r in range(0, out.shape[0], rows):
        lhs = [adj[r : r + rows, at : at + part.shape[0]] for at, part in zip(starts, parts)]
        value = jnp.dot(jnp.concatenate(lhs, axis=1), rhs, preferred_element_type=F32)
        if start is not None:
            value = value + start[r : r + rows, :]
        out[r : r + rows, :] = value.astype(out.dtype)


def gather_matmul(adj, parts, start, dtype, name):
    starts = [(core * NY + dy) * NZH * TILE + first for core, dy, first, _ in parts]
    parts = [part for *_, part in parts]
    rows, width = adj.shape[0], parts[0].shape[1]
    operands = [adj, *parts] + ([] if start is None else [start])
    return in_vmem(functools.partial(gather_kernel, starts), [kept((rows, width), dtype)], operands, name)[0]


def node_kernel(parts, base, degf_row, w_neigh, cotangent, grad, scaled_t, out):
    total = parts[0:TILE, :].astype(F32)
    for i in range(1, NCOL):
        total = total + parts[i * TILE : (i + 1) * TILE, :].astype(F32)
    degf_col = jnp.broadcast_to(degf_row[...], (TILE, TILE)).T[:, :1]
    mean = (total / degf_col).astype(BF16)
    pre = base[...] + jnp.dot(mean, w_neigh[...], preferred_element_type=F32)
    sig = jax.nn.sigmoid(pre)
    out[...] = (pre * sig).astype(BF16)
    slope = sig * (1.0 + pre * (1.0 - sig))
    grad_pre = (cotangent[...].astype(F32) * slope).astype(BF16)
    grad[...] = grad_pre
    proj_t = lax.dot_general(w_neigh[...], grad_pre, (((1,), (1,)), ((), ())), preferred_element_type=F32)
    scaled = (proj_t / degf_row[...]).astype(BF16)
    for i in range(NCOL):
        scaled_t[i, :, :] = scaled


def node_step(parts, base, degf_row, w_neigh, cotangent):
    rows, width = cotangent.shape
    results = [kept((rows, width), BF16), kept((NCOL, width, rows), BF16), plain((rows, width), BF16)]
    operands = (parts, base, degf_row, w_neigh, cotangent)
    return in_vmem(node_kernel, results, operands, "node_step", 4 * rows * width * width)


def spread_kernel(core, dys, parts, adj, *outs):
    lhs = jnp.concatenate([parts[i] for i in range(NCOL)], axis=1)
    depth = NZH * TILE
    for i, dy in enumerate(dys):
        at = (core * NY + dy) * depth
        value = jnp.dot(lhs, adj[:, at : at + depth], preferred_element_type=F32)
        outs[0][i] = value.astype(BF16)


def spread_matmul(parts, adj, core, dys, name):
    shape = (len(dys), parts.shape[1], NZH * TILE)
    return in_vmem(functools.partial(spread_kernel, core, dys), [kept(shape, BF16)], (parts, adj), name)[0]


def far_sum_kernel(mine, theirs, left, right):
    half = left.shape[0]
    value = mine[0].astype(F32) + theirs[0].astype(F32)
    left[...] = value[:half].astype(BF16)
    right[...] = value[half:].astype(BF16)


def far_sum(mine, theirs):
    shape = (mine.shape[1] // 2, mine.shape[2])
    return in_vmem(far_sum_kernel, [kept(shape, BF16)] * 2, (mine, theirs), "far_sum")


def near_sum_kernel(mine, theirs, left, right, one, three):
    half = left.shape[0]
    first = mine[0].astype(F32) + theirs[0].astype(F32)
    one[:half] = (first[:half] + left[...].astype(F32)).astype(BF16)
    one[half:] = first[half:].astype(BF16)
    second = mine[1].astype(F32) + theirs[1].astype(F32)
    three[:half] = second[:half].astype(BF16)
    three[half:] = (second[half:] + right[...].astype(F32)).astype(BF16)


def near_sum(mine, theirs, left, right):
    return in_vmem(near_sum_kernel, [kept(mine.shape[1:], BF16)] * 2, (mine, theirs, left, right), "near_sum")


def plane_sum_kernel(mine, theirs, one, three, near, left, right):
    value = mine[0].astype(F32) + theirs[0].astype(F32) + one[...].astype(F32) + three[...].astype(F32)
    half = left.shape[0]
    for i, tile in enumerate(RING[:3]):
        near[i] = value[:, tile * TILE : (tile + 1) * TILE]
    far = value[:, RING[3] * TILE : (RING[3] + 1) * TILE].astype(BF16)
    left[...] = far[:half]
    right[...] = far[half:]


def plane_sum(mine, theirs, one, three):
    width = mine.shape[1]
    results = [kept((3, width, TILE), F32)] + [kept((width // 2, TILE), BF16)] * 2
    return in_vmem(plane_sum_kernel, results, (mine, theirs, one, three), "plane_sum")


def tile_sum_kernel(near, left, right, one, three):
    half = left.shape[0]
    one[:half] = (near[1, :half] + left[...].astype(F32)).astype(BF16)
    one[half:] = near[1, half:].astype(BF16)
    three[:half] = near[2, :half].astype(BF16)
    three[half:] = (near[2, half:] + right[...].astype(F32)).astype(BF16)


def tile_sum(near, left, right):
    return in_vmem(tile_sum_kernel, [kept(near.shape[1:], BF16)] * 2, (near, left, right), "tile_sum")


def last_kernel(near, one, three, own, out):
    back = near[0] + one[...].astype(F32) + three[...].astype(F32)
    out[...] = (own[...] + back.T).astype(BF16)


def last_sum(near, one, three, own):
    return in_vmem(last_kernel, [plain(own.shape, BF16)], (near, one, three, own), "last_sum")[0]


def body(features, degrees, tile_rows, tile_masks, w_self, w_neigh, bias, cotangent):
    row = lax.axis_index("row").astype(jnp.int32)

    differ = jnp.arange(NROW, dtype=jnp.int32) ^ row
    adj = adjacency(tile_masks[0, 0], (differ % NCORE) * CHIPS + differ // NCORE, tile_rows[0, 0].reshape(-1))
    degf_row = degrees.astype(F32)[None, :]
    base = jnp.dot(features, w_self, preferred_element_type=F32) + bias[None, :]

    half = TILE // 2
    z1, z3 = flip(features, z=1), flip(features, z=3)
    z2 = [flip(z1[:half], z=3), flip(z3[half:], z=1)]
    plane = jnp.concatenate([features, z1, *z2, z3], axis=0)
    half = plane.shape[0] // 2
    y1, y3 = flip(plane, y=1), flip(plane, y=3)
    plane, adj, base, degf_row = lax.optimization_barrier((plane, adj, base, degf_row))
    other = flip(plane, core=1)
    part = gather_matmul(adj, [(0, 0, 0, plane), (1, 0, 0, other)], None, F32, "gather_plane")
    y1, y3, part = lax.optimization_barrier((y1, y3, part))
    y2 = [flip(y1[:half], y=3), flip(y3[half:], y=1)]
    o1, o3 = flip(y1, core=1), flip(y3, core=1)
    part = gather_matmul(adj, [(0, 1, 0, y1), (0, 3, 0, y3), (1, 1, 0, o1), (1, 3, 0, o3)], part, F32, "gather_near")
    *y2, part = lax.optimization_barrier((*y2, part))
    o2 = [flip(v, core=1) for v in y2]
    part = gather_matmul(adj, [(0, 2, 0, y2[0]), (0, 2, half, y2[1])], part, F32, "gather_far")
    *o2, part = lax.optimization_barrier((*o2, part))
    summed = gather_matmul(adj, [(1, 2, 0, o2[0]), (1, 2, half, o2[1])], part, BF16, "gather_far_other")

    arrived = lax.all_to_all(summed, "col", 0, 0, tiled=True)
    grad_pre, scaled_t, output = node_step(arrived, base, degf_row, w_neigh, cotangent)

    table = lax.all_to_all(scaled_t, "col", 0, 0, tiled=True)
    own = lax.dot_general(grad_pre, w_self, (((1,), (1,)), ((), ())), preferred_element_type=F32)

    theirs = flip(spread_matmul(table, adj, 1, (2,), "spread_far_other"), core=1)
    mine = spread_matmul(table, adj, 0, (2,), "spread_far")
    near_other = spread_matmul(table, adj, 1, (1, 3), "spread_near_other")
    theirs, mine, near_other = lax.optimization_barrier((theirs, mine, near_other))
    left, right = far_sum(mine, theirs)
    left, right, table = lax.optimization_barrier((left, right, table))
    left, right = flip(left, y=3), flip(right, y=1)
    mine = spread_matmul(table, adj, 0, (1, 3), "spread_near")
    theirs = flip(near_other, core=1)
    left, right, mine = lax.optimization_barrier((left, right, mine))
    one, three = near_sum(mine, theirs, left, right)
    one, three, table = lax.optimization_barrier((one, three, table))
    one, three = flip(one, y=1), flip(three, y=3)
    theirs = flip(spread_matmul(table, adj, 1, (0,), "spread_plane_other"), core=1)
    mine = spread_matmul(table, adj, 0, (0,), "spread_plane")
    one, three, mine = lax.optimization_barrier((one, three, mine))
    near, left, right = plane_sum(mine, theirs, one, three)
    left, right = flip(left, z=3), flip(right, z=1)
    one, three = tile_sum(near, left, right)
    grad_features = last_sum(near, flip(one, z=1), flip(three, z=3), own)
    return output, grad_features


def solution(mesh):
    both = P(("row", "col"), None)
    return jax.shard_map(
        body,
        mesh=mesh,
        in_specs=(
            both,
            P(("row", "col")),
            P("row", "col", None, None),
            P("row", "col", None, None, None, None),
            P(),
            P(),
            P(),
            both,
        ),
        out_specs=(both, both),
        check_vma=False,
    )
```

```python
import functools

import jax
import jax.numpy as jnp
from jax import lax
from jax.experimental import pallas as pl
from jax.experimental.pallas import tpu as pltpu
from jax.sharding import PartitionSpec as P

NY, NZH, NCORE, NX, NZL = 4, 4, 2, 4, 2
NROW, NCOL = NY * NZH * NCORE, NX * NZL
CHIPS = NY * NZH
STEPS = ((1, 3), (3, 1))
TILE = 128
BF16 = jnp.bfloat16
F32 = jnp.float32
MB = 1024 * 1024


def exchange(value, axis, step):
    pairs = []
    for row in range(NROW):
        bits = STEPS[row % NCORE][step]
        there = row ^ ((bits * NZH if axis == "y" else bits) * NCORE)
        pairs += [(row * NCOL + col, there * NCOL + col) for col in range(NCOL)]
    return lax.ppermute(value, ("row", "col"), pairs)


def swap(value):
    pairs = [(row * NCOL + col, (row ^ 1) * NCOL + col) for row in range(NROW) for col in range(NCOL)]
    return lax.ppermute(value, ("row", "col"), pairs)


def in_vmem(kernel, results, operands, name, flops=MB, grant=16, **extra):
    spec = pl.BlockSpec(memory_space=pltpu.VMEM)
    outs = [shape if plain else pltpu.VMEM(shape.shape, shape.dtype) for shape, plain in results]
    out_specs = [pl.BlockSpec() if plain else spec for _, plain in results]
    return pl.pallas_call(
        kernel,
        in_specs=[spec] * len(operands),
        out_specs=out_specs,
        out_shape=outs,
        compiler_params=pltpu.CompilerParams(vmem_limit_bytes=grant * MB),
        cost_estimate=pl.CostEstimate(flops=0, bytes_accessed=1024, transcendentals=0),
        name=name,
        **extra,
    )(*[pltpu.with_memory_space_constraint(v, pltpu.VMEM) for v in operands])


def kept(shape, dtype):
    return jax.ShapeDtypeStruct(shape, dtype), False


def plain(shape, dtype):
    return jax.ShapeDtypeStruct(shape, dtype), True


def adjacency_kernel(place, where, masks, out, held, sems):
    count, slots = masks.shape[0], masks.shape[1]
    copies = [pltpu.make_async_copy(masks.at[j], held.at[j], sems.at[j]) for j in range(count)]
    for copy in copies:
        copy.start()
    for j, copy in enumerate(copies):
        cols = pl.ds(pl.multiple_of(place[j] * TILE, TILE), TILE)
        out[:, cols] = jnp.zeros((out.shape[0], TILE), BF16)
        copy.wait()
        for k in range(slots):
            at = pl.ds(pl.multiple_of(where[j * slots + k] * TILE, TILE), TILE)
            out[at, cols] = out[at, cols] + held[j, k].astype(F32).astype(BF16)


def adjacency(masks, place, where):
    count = masks.shape[0]
    return pl.pallas_call(
        adjacency_kernel,
        grid_spec=pltpu.PrefetchScalarGridSpec(
            num_scalar_prefetch=2,
            grid=(1,),
            in_specs=[pl.BlockSpec(memory_space=pl.ANY)],
            out_specs=pl.BlockSpec(memory_space=pltpu.VMEM),
            scratch_shapes=[pltpu.VMEM(masks.shape, masks.dtype), pltpu.SemaphoreType.DMA((count,))],
        ),
        out_shape=pltpu.VMEM((NCOL * TILE, count * TILE), BF16),
        compiler_params=pltpu.CompilerParams(vmem_limit_bytes=16 * MB),
        cost_estimate=pl.CostEstimate(flops=0, bytes_accessed=14 * MB, transcendentals=0),
        name="adjacency",
    )(place, where, pltpu.with_memory_space_constraint(masks, pltpu.HBM))


def gather_kernel(starts, adj, *refs):
    parts, out = refs[: len(starts)], refs[-1]
    start = refs[-2] if len(refs) > len(parts) + 1 else None
    rows = 2 * TILE
    rhs = jnp.concatenate([part[...] for part in parts], axis=0)
    for r in range(0, out.shape[0], rows):
        lhs = [adj[r : r + rows, at : at + part.shape[0]] for at, part in zip(starts, parts)]
        value = jnp.dot(jnp.concatenate(lhs, axis=1), rhs, preferred_element_type=F32)
        if start is not None:
            value = value + start[r : r + rows, :]
        out[r : r + rows, :] = value.astype(out.dtype)


def gather_matmul(adj, parts, start, dtype, name):
    starts = [(core * 2 + half) * CHIPS // 2 * TILE for core, half, _ in parts]
    parts = [part for *_, part in parts]
    rows, width = adj.shape[0], parts[0].shape[1]
    operands = [adj, *parts] + ([] if start is None else [start])
    return in_vmem(functools.partial(gather_kernel, starts), [kept((rows, width), dtype)], operands, name)[0]


def node_kernel(parts, base, degf_row, w_neigh, cotangent, grad, scaled_t, out):
    total = parts[0:TILE, :].astype(F32)
    for i in range(1, NCOL):
        total = total + parts[i * TILE : (i + 1) * TILE, :].astype(F32)
    degf_col = jnp.broadcast_to(degf_row[...], (TILE, TILE)).T[:, :1]
    mean = (total / degf_col).astype(BF16)
    pre = base[...] + jnp.dot(mean, w_neigh[...], preferred_element_type=F32)
    sig = jax.nn.sigmoid(pre)
    out[...] = (pre * sig).astype(BF16)
    slope = sig * (1.0 + pre * (1.0 - sig))
    grad_pre = (cotangent[...].astype(F32) * slope).astype(BF16)
    grad[...] = grad_pre
    proj_t = lax.dot_general(w_neigh[...], grad_pre, (((1,), (1,)), ((), ())), preferred_element_type=F32)
    scaled = (proj_t / degf_row[...]).astype(BF16)
    for i in range(NCOL):
        scaled_t[i, :, :] = scaled


def node_step(parts, base, degf_row, w_neigh, cotangent):
    rows, width = cotangent.shape
    results = [kept((rows, width), BF16), kept((NCOL, width, rows), BF16), plain((rows, width), BF16)]
    operands = (parts, base, degf_row, w_neigh, cotangent)
    return in_vmem(node_kernel, results, operands, "node_step", 4 * rows * width * width)


def spread_kernel(first, parts, adj, out):
    lhs = jnp.concatenate([parts[i] for i in range(NCOL)], axis=1)
    depth = NZH * TILE
    for at in range(0, out.shape[1], depth):
        value = jnp.dot(lhs, adj[:, first + at : first + at + depth], preferred_element_type=F32)
        out[:, at : at + depth] = value.astype(BF16)


def spread_matmul(parts, adj, core, half, name):
    shape = (parts.shape[1], CHIPS // 2 * TILE)
    first = (core * 2 + half) * shape[1]
    return in_vmem(functools.partial(spread_kernel, first), [kept(shape, BF16)], (parts, adj), name)[0]


def sum_kernel(*refs):
    value = refs[0][...].astype(F32)
    for ref in refs[1:-1]:
        value = value + ref[...].astype(F32)
    refs[-1][...] = value.astype(BF16)


def pair_sum(mine, theirs):
    return in_vmem(sum_kernel, [kept(mine.shape, BF16)], (mine, theirs), "pair_sum")[0]


def split_kernel(*refs):
    value = refs[0][...].astype(F32)
    for ref in refs[1:-2]:
        value = value + ref[...].astype(F32)
    stay, go = refs[-2:]
    half = stay.shape[1]
    stay[...] = value[:, :half]
    go[...] = value[:, half:].astype(BF16)


def split_sum(values, name):
    rows, cols = values[0].shape
    results = [kept((rows, cols // 2), F32), kept((rows, cols // 2), BF16)]
    return in_vmem(split_kernel, results, values, name)


def last_kernel(stay, got, own, out):
    back = stay[...] + got[...].astype(F32)
    out[...] = (own[...] + back.T).astype(BF16)


def last_sum(stay, got, own):
    return in_vmem(last_kernel, [plain(own.shape, BF16)], (stay, got, own), "last_sum")[0]


def body(features, degrees, tile_rows, tile_masks, w_self, w_neigh, bias, cotangent):
    row = lax.axis_index("row").astype(jnp.int32)

    device = jnp.arange(NROW, dtype=jnp.int32)
    differ = device ^ row
    bits = [(differ // (NZH * NCORE)) % NY, (differ // NCORE) % NZH]
    turn = []
    for d in bits:
        by_core = [jnp.where(d == k1, 1, jnp.where(d == k2, 2, jnp.where(d == 0, 0, 3))) for k1, k2 in STEPS]
        turn.append(jnp.where(device % NCORE == 0, *by_core))
    place = (differ % NCORE) * CHIPS + turn[0] * NZH + turn[1]
    adj = adjacency(tile_masks[0, 0], place.astype(jnp.int32), tile_rows[0, 0].reshape(-1))
    degf_row = degrees.astype(F32)[None, :]
    base = jnp.dot(features, w_self, preferred_element_type=F32) + bias[None, :]

    pair = jnp.concatenate([features, exchange(features, "z", 0)], axis=0)
    plane = jnp.concatenate([pair, exchange(pair, "z", 1)], axis=0)
    got = exchange(plane, "y", 0)
    got, adj, base, degf_row = lax.optimization_barrier((got, adj, base, degf_row))
    near = jnp.concatenate([plane, got], axis=0)
    far = exchange(near, "y", 1)
    part = gather_matmul(adj, [(0, 0, near), (1, 0, swap(near))], None, F32, "gather_near")
    far, part = lax.optimization_barrier((far, part))
    other = swap(far)
    part = gather_matmul(adj, [(0, 1, far)], part, F32, "gather_far")
    other, part = lax.optimization_barrier((other, part))
    summed = gather_matmul(adj, [(1, 1, other)], part, BF16, "gather_far_other")

    arrived = lax.all_to_all(summed, "col", 0, 0, tiled=True)
    grad_pre, scaled_t, output = node_step(arrived, base, degf_row, w_neigh, cotangent)

    table = lax.all_to_all(scaled_t, "col", 0, 0, tiled=True)
    own = lax.dot_general(grad_pre, w_self, (((1,), (1,)), ((), ())), preferred_element_type=F32)

    theirs = swap(spread_matmul(table, adj, 1, 1, "spread_far_other"))
    mine = spread_matmul(table, adj, 0, 1, "spread_far")
    near_other = spread_matmul(table, adj, 1, 0, "spread_near_other")
    theirs, mine, near_other = lax.optimization_barrier((theirs, mine, near_other))
    value = pair_sum(mine, theirs)
    value, table = lax.optimization_barrier((value, table))
    got = exchange(value, "y", 1)
    theirs = swap(near_other)
    mine = spread_matmul(table, adj, 0, 0, "spread_near")
    got, mine = lax.optimization_barrier((got, mine))
    stay, go = split_sum((mine, theirs, got), "sum_y1")
    stay, go = split_sum((stay, exchange(go, "y", 0)), "sum_y0")
    stay, go = split_sum((stay, exchange(go, "z", 1)), "sum_z1")
    grad_features = last_sum(stay, exchange(go, "z", 0), own)
    return output, grad_features


def solution(mesh):
    both = P(("row", "col"), None)
    return jax.shard_map(
        body,
        mesh=mesh,
        in_specs=(
            both,
            P(("row", "col")),
            P("row", "col", None, None),
            P("row", "col", None, None, None, None),
            P(),
            P(),
            P(),
            both,
        ),
        out_specs=(both, both),
        check_vma=False,
    )
```

```python
import functools

import jax
import jax.numpy as jnp
from jax import lax
from jax.experimental import pallas as pl
from jax.experimental.pallas import tpu as pltpu
from jax.sharding import PartitionSpec as P

NY, NZH, NCORE, NX, NZL = 4, 4, 2, 4, 2
NROW, NCOL = NY * NZH * NCORE, NX * NZL
CHIPS = NY * NZH
STEPS = ((1, 3), (3, 1))
TILE = 128
BF16 = jnp.bfloat16
F32 = jnp.float32
MB = 1024 * 1024


def exchange(value, axis, step):
    pairs = []
    for row in range(NROW):
        bits = STEPS[row % NCORE][step]
        there = row ^ ((bits * NZH if axis == "y" else bits) * NCORE)
        pairs += [(row * NCOL + col, there * NCOL + col) for col in range(NCOL)]
    return lax.ppermute(value, ("row", "col"), pairs)


def swap(value):
    pairs = [(row * NCOL + col, (row ^ 1) * NCOL + col) for row in range(NROW) for col in range(NCOL)]
    return lax.ppermute(value, ("row", "col"), pairs)


def in_vmem(kernel, results, operands, name, flops=MB, grant=16, **extra):
    spec = pl.BlockSpec(memory_space=pltpu.VMEM)
    outs = [shape if plain else pltpu.VMEM(shape.shape, shape.dtype) for shape, plain in results]
    out_specs = [pl.BlockSpec() if plain else spec for _, plain in results]
    return pl.pallas_call(
        kernel,
        in_specs=[spec] * len(operands),
        out_specs=out_specs,
        out_shape=outs,
        compiler_params=pltpu.CompilerParams(vmem_limit_bytes=grant * MB),
        cost_estimate=pl.CostEstimate(flops=0, bytes_accessed=1024, transcendentals=0),
        name=name,
        **extra,
    )(*[pltpu.with_memory_space_constraint(v, pltpu.VMEM) for v in operands])


def kept(shape, dtype):
    return jax.ShapeDtypeStruct(shape, dtype), False


def plain(shape, dtype):
    return jax.ShapeDtypeStruct(shape, dtype), True


def adjacency_kernel(place, where, masks, out, held, sems):
    count, slots = masks.shape[0], masks.shape[1]
    copies = [pltpu.make_async_copy(masks.at[j], held.at[j], sems.at[j]) for j in range(count)]
    for copy in copies:
        copy.start()
    for j, copy in enumerate(copies):
        cols = pl.ds(pl.multiple_of(place[j] * TILE, TILE), TILE)
        out[:, cols] = jnp.zeros((out.shape[0], TILE), BF16)
        copy.wait()
        for k in range(slots):
            at = pl.ds(pl.multiple_of(where[j * slots + k] * TILE, TILE), TILE)
            out[at, cols] = out[at, cols] + held[j, k].astype(F32).astype(BF16)


def adjacency(masks, place, where):
    count = masks.shape[0]
    return pl.pallas_call(
        adjacency_kernel,
        grid_spec=pltpu.PrefetchScalarGridSpec(
            num_scalar_prefetch=2,
            grid=(1,),
            in_specs=[pl.BlockSpec(memory_space=pl.ANY)],
            out_specs=pl.BlockSpec(memory_space=pltpu.VMEM),
            scratch_shapes=[pltpu.VMEM(masks.shape, masks.dtype), pltpu.SemaphoreType.DMA((count,))],
        ),
        out_shape=pltpu.VMEM((NCOL * TILE, count * TILE), BF16),
        compiler_params=pltpu.CompilerParams(vmem_limit_bytes=16 * MB),
        cost_estimate=pl.CostEstimate(flops=0, bytes_accessed=14 * MB, transcendentals=0),
        name="adjacency",
    )(place, where, pltpu.with_memory_space_constraint(masks, pltpu.HBM))


def halves_kernel(first, second, *outs):
    rows = first.shape[0]
    width = outs[0].shape[1]
    for w, out in enumerate(outs):
        out[:rows, :] = first[:, w * width : (w + 1) * width]
        out[rows:, :] = second[:, w * width : (w + 1) * width]


def join(first, second, count, name):
    shape = (2 * first.shape[0], first.shape[1] // count)
    return in_vmem(halves_kernel, [kept(shape, BF16)] * count, (first, second), name)


def gather_kernel(starts, adj, *refs):
    parts, out = refs[: 2 * len(starts)], refs[-1]
    start = refs[-2] if len(refs) > len(parts) + 1 else None
    rows = 2 * TILE
    rhs = [jnp.concatenate([parts[i][...], parts[i + 1][...]], axis=1) for i in range(0, len(parts), 2)]
    rhs = jnp.concatenate(rhs, axis=0)
    depth = parts[0].shape[0]
    for r in range(0, out.shape[0], rows):
        lhs = [adj[r : r + rows, at : at + depth] for at in starts]
        value = jnp.dot(jnp.concatenate(lhs, axis=1), rhs, preferred_element_type=F32)
        if start is not None:
            value = value + start[r : r + rows, :]
        out[r : r + rows, :] = value.astype(out.dtype)


def gather_matmul(adj, parts, start, dtype, name):
    starts = [(core * 2 + half) * CHIPS // 2 * TILE for core, half, _ in parts]
    arrays = [wave for *_, waves in parts for wave in waves]
    rows, width = adj.shape[0], 2 * arrays[0].shape[1]
    operands = [adj, *arrays] + ([] if start is None else [start])
    return in_vmem(functools.partial(gather_kernel, starts), [kept((rows, width), dtype)], operands, name)[0]


def node_kernel(parts, base, degf_row, w_neigh, cotangent, grad, scaled_t, out):
    total = parts[0:TILE, :].astype(F32)
    for i in range(1, NCOL):
        total = total + parts[i * TILE : (i + 1) * TILE, :].astype(F32)
    degf_col = jnp.broadcast_to(degf_row[...], (TILE, TILE)).T[:, :1]
    mean = (total / degf_col).astype(BF16)
    pre = base[...] + jnp.dot(mean, w_neigh[...], preferred_element_type=F32)
    sig = jax.nn.sigmoid(pre)
    out[...] = (pre * sig).astype(BF16)
    slope = sig * (1.0 + pre * (1.0 - sig))
    grad_pre = (cotangent[...].astype(F32) * slope).astype(BF16)
    grad[...] = grad_pre
    proj_t = lax.dot_general(w_neigh[...], grad_pre, (((1,), (1,)), ((), ())), preferred_element_type=F32)
    scaled = (proj_t / degf_row[...]).astype(BF16)
    for i in range(NCOL):
        scaled_t[i, :, :] = scaled


def node_step(parts, base, degf_row, w_neigh, cotangent):
    rows, width = cotangent.shape
    results = [kept((rows, width), BF16), kept((NCOL, width, rows), BF16), plain((rows, width), BF16)]
    operands = (parts, base, degf_row, w_neigh, cotangent)
    return in_vmem(node_kernel, results, operands, "node_step", 4 * rows * width * width)


def spread_kernel(first, parts, adj, *outs):
    lhs = jnp.concatenate([parts[i] for i in range(NCOL)], axis=1)
    depth = NZH * TILE
    rows, cols = outs[0].shape
    for at in range(0, cols, depth):
        value = jnp.dot(lhs, adj[:, first + at : first + at + depth], preferred_element_type=F32).astype(BF16)
        for w, out in enumerate(outs):
            out[:, at : at + depth] = value[w * rows : (w + 1) * rows, :]


def spread_matmul(parts, adj, core, half, name):
    shape = (parts.shape[1] // 2, CHIPS // 2 * TILE)
    first = (core * 2 + half) * shape[1]
    return in_vmem(functools.partial(spread_kernel, first), [kept(shape, BF16)] * 2, (parts, adj), name)


def sum_kernel(*refs):
    value = refs[0][...].astype(F32)
    for ref in refs[1:-1]:
        value = value + ref[...].astype(F32)
    refs[-1][...] = value.astype(BF16)


def pair_sum(mine, theirs):
    return in_vmem(sum_kernel, [kept(mine.shape, BF16)], (mine, theirs), "pair_sum")[0]


def split_kernel(*refs):
    value = refs[0][...].astype(F32)
    for ref in refs[1:-2]:
        value = value + ref[...].astype(F32)
    stay, go = refs[-2:]
    half = stay.shape[1]
    stay[...] = value[:, :half]
    go[...] = value[:, half:].astype(BF16)


def split_sum(values, name):
    rows, cols = values[0].shape
    results = [kept((rows, cols // 2), F32), kept((rows, cols // 2), BF16)]
    return in_vmem(split_kernel, results, values, name)


def last_kernel(*refs):
    waves, own, out = refs[:-2], refs[-2], refs[-1]
    back = [waves[i][...] + waves[i + 1][...].astype(F32) for i in range(0, len(waves), 2)]
    out[...] = (own[...] + jnp.concatenate(back, axis=0).T).astype(BF16)


def last_sum(waves, own):
    return in_vmem(last_kernel, [plain(own.shape, BF16)], (*waves, own), "last_sum")[0]


def body(features, degrees, tile_rows, tile_masks, w_self, w_neigh, bias, cotangent):
    row = lax.axis_index("row").astype(jnp.int32)

    device = jnp.arange(NROW, dtype=jnp.int32)
    differ = device ^ row
    bits = [(differ // (NZH * NCORE)) % NY, (differ // NCORE) % NZH]
    turn = []
    for d in bits:
        by_core = [jnp.where(d == k1, 1, jnp.where(d == k2, 2, jnp.where(d == 0, 0, 3))) for k1, k2 in STEPS]
        turn.append(jnp.where(device % NCORE == 0, *by_core))
    place = (differ % NCORE) * CHIPS + turn[0] * NZH + turn[1]
    adj = adjacency(tile_masks[0, 0], place.astype(jnp.int32), tile_rows[0, 0].reshape(-1))
    degf_row = degrees.astype(F32)[None, :]
    base = jnp.dot(features, w_self, preferred_element_type=F32) + bias[None, :]

    got, adj = lax.optimization_barrier((exchange(features, "z", 0), adj))
    waves = join(features, got, 2, "join_z0")
    got = [exchange(v, "z", 1) for v in waves]
    waves = [join(v, g, 1, "join_z1")[0] for v, g in zip(waves, got)]
    got = [exchange(v, "y", 0) for v in waves]
    got[1], base, degf_row = lax.optimization_barrier((got[1], base, degf_row))
    near = [join(v, g, 1, "join_y0")[0] for v, g in zip(waves, got)]
    far = [exchange(v, "y", 1) for v in near]
    other = [swap(v) for v in near]
    part = gather_matmul(adj, [(0, 0, near), (1, 0, other)], None, F32, "gather_near")
    *far, part = lax.optimization_barrier((*far, part))
    other = [swap(v) for v in far]
    part = gather_matmul(adj, [(0, 1, far)], part, F32, "gather_far")
    *other, part = lax.optimization_barrier((*other, part))
    summed = gather_matmul(adj, [(1, 1, other)], part, BF16, "gather_far_other")

    arrived = lax.all_to_all(summed, "col", 0, 0, tiled=True)
    grad_pre, scaled_t, output = node_step(arrived, base, degf_row, w_neigh, cotangent)

    table = lax.all_to_all(scaled_t, "col", 0, 0, tiled=True)
    own = lax.dot_general(grad_pre, w_self, (((1,), (1,)), ((), ())), preferred_element_type=F32)

    theirs = [swap(v) for v in spread_matmul(table, adj, 1, 1, "spread_far_other")]
    mine = spread_matmul(table, adj, 0, 1, "spread_far")
    near_other = spread_matmul(table, adj, 1, 0, "spread_near_other")
    *theirs, table = lax.optimization_barrier((*theirs, *mine, *near_other, table))
    theirs, mine, near_other = theirs[:2], theirs[2:4], theirs[4:]
    values = [pair_sum(a, b) for a, b in zip(mine, theirs)]
    values[0], table = lax.optimization_barrier((values[0], table))
    got = [exchange(v, "y", 1) for v in values]
    theirs = [swap(v) for v in near_other]
    mine = spread_matmul(table, adj, 0, 0, "spread_near")
    got[0], *mine = lax.optimization_barrier((got[0], *mine))
    ends = []
    for w in range(2):
        stay, go = split_sum((mine[w], theirs[w], got[w]), "sum_y1")
        stay, go = split_sum((stay, exchange(go, "y", 0)), "sum_y0")
        stay, go = split_sum((stay, exchange(go, "z", 1)), "sum_z1")
        ends += [stay, exchange(go, "z", 0)]
    grad_features = last_sum(ends, own)
    return output, grad_features


def solution(mesh):
    both = P(("row", "col"), None)
    return jax.shard_map(
        body,
        mesh=mesh,
        in_specs=(
            both,
            P(("row", "col")),
            P("row", "col", None, None),
            P("row", "col", None, None, None, None),
            P(),
            P(),
            P(),
            both,
        ),
        out_specs=(both, both),
        check_vma=False,
    )
```

```python
import functools

import jax
import jax.numpy as jnp
from jax import lax
from jax.experimental import pallas as pl
from jax.experimental.pallas import tpu as pltpu
from jax.sharding import PartitionSpec as P

NY, NZH, NCORE, NX, NZL = 4, 4, 2, 4, 2
NROW, NCOL = NY * NZH * NCORE, NX * NZL
CHIPS = NY * NZH
STEPS = ((1, 3), (3, 1))
TILE = 128
AXES = (("z", "y"), ("y", "z"))
SPLIT = 320
BF16 = jnp.bfloat16
F32 = jnp.float32
MB = 1024 * 1024


def exchange(value, axis, step):
    pairs = []
    for row in range(NROW):
        bits = STEPS[row % NCORE][step]
        there = row ^ ((bits * NZH if axis == "y" else bits) * NCORE)
        pairs += [(row * NCOL + col, there * NCOL + col) for col in range(NCOL)]
    return lax.ppermute(value, ("row", "col"), pairs)


def swap(value):
    pairs = [(row * NCOL + col, (row ^ 1) * NCOL + col) for row in range(NROW) for col in range(NCOL)]
    return lax.ppermute(value, ("row", "col"), pairs)


def in_vmem(kernel, results, operands, name, flops=MB, grant=16, **extra):
    spec = pl.BlockSpec(memory_space=pltpu.VMEM)
    outs = [shape if plain else pltpu.VMEM(shape.shape, shape.dtype) for shape, plain in results]
    out_specs = [pl.BlockSpec() if plain else spec for _, plain in results]
    return pl.pallas_call(
        kernel,
        in_specs=[spec] * len(operands),
        out_specs=out_specs,
        out_shape=outs,
        compiler_params=pltpu.CompilerParams(vmem_limit_bytes=grant * MB),
        cost_estimate=pl.CostEstimate(flops=0, bytes_accessed=1024, transcendentals=0),
        name=name,
        **extra,
    )(*[pltpu.with_memory_space_constraint(v, pltpu.VMEM) for v in operands])


def kept(shape, dtype):
    return jax.ShapeDtypeStruct(shape, dtype), False


def plain(shape, dtype):
    return jax.ShapeDtypeStruct(shape, dtype), True


def adjacency_kernel(place, where, masks, out, held, sems):
    count, slots = masks.shape[0], masks.shape[1]
    copies = [pltpu.make_async_copy(masks.at[j], held.at[j], sems.at[j]) for j in range(count)]
    for copy in copies:
        copy.start()
    for j, copy in enumerate(copies):
        cols = pl.ds(pl.multiple_of(place[j] * TILE, TILE), TILE)
        out[:, cols] = jnp.zeros((out.shape[0], TILE), BF16)
        copy.wait()
        for k in range(slots):
            at = pl.ds(pl.multiple_of(where[j * slots + k] * TILE, TILE), TILE)
            out[at, cols] = out[at, cols] + held[j, k].astype(F32).astype(BF16)


def adjacency(masks, place, where):
    count = masks.shape[0]
    return pl.pallas_call(
        adjacency_kernel,
        grid_spec=pltpu.PrefetchScalarGridSpec(
            num_scalar_prefetch=2,
            grid=(1,),
            in_specs=[pl.BlockSpec(memory_space=pl.ANY)],
            out_specs=pl.BlockSpec(memory_space=pltpu.VMEM),
            scratch_shapes=[pltpu.VMEM(masks.shape, masks.dtype), pltpu.SemaphoreType.DMA((count,))],
        ),
        out_shape=pltpu.VMEM((NCOL * TILE, count * TILE), BF16),
        compiler_params=pltpu.CompilerParams(vmem_limit_bytes=16 * MB),
        cost_estimate=pl.CostEstimate(flops=0, bytes_accessed=14 * MB, transcendentals=0),
        name="adjacency",
    )(place, where, pltpu.with_memory_space_constraint(masks, pltpu.HBM))


def tiles_of(wave, core, half):
    out = []
    for n in range(half * CHIPS // 2, (half + 1) * CHIPS // 2):
        slow, fast = n // NZH, n % NZH
        out.append(core * CHIPS + (slow * NZH + fast if wave == 0 else fast * NZH + slow))
    return out


def columns(adj, rows, tiles):
    pieces = []
    for tile in tiles:
        if pieces and pieces[-1][1] == tile:
            pieces[-1][1] = tile + 1
        else:
            pieces.append([tile, tile + 1])
    parts = [adj[rows, a * TILE : b * TILE] for a, b in pieces]
    return parts[0] if len(parts) == 1 else jnp.concatenate(parts, axis=1)


def join_kernel(at, first, second, out):
    rows, width = first.shape[0], out.shape[1]
    out[:rows, :] = first[:, at : at + width]
    out[rows:, :] = second[:, at : at + width]


def join(first, second, at, width, name):
    shape = (2 * first.shape[0], width)
    return in_vmem(functools.partial(join_kernel, at), [kept(shape, BF16)], (first, second), name)[0]


def gather_kernel(parts, adj, *refs):
    out = refs[-1]
    start = refs[-2] if len(refs) > 2 * len(parts) + 1 else None
    width = out.shape[1] // 2
    step = 2 * TILE
    for w in range(2):
        cols = slice(w * width, (w + 1) * width)
        rhs = jnp.concatenate([refs[2 * i + w][...] for i in range(len(parts))], axis=0)
        tiles = [tile for core, half in parts for tile in tiles_of(w, core, half)]
        for r in range(0, out.shape[0], step):
            rows = slice(r, r + step)
            value = jnp.dot(columns(adj, rows, tiles), rhs, preferred_element_type=F32)
            if start is not None:
                value = value + start[rows, cols]
            out[rows, cols] = value.astype(out.dtype)


def gather_matmul(adj, parts, start, dtype, name):
    which = [(core, half) for core, half, _ in parts]
    arrays = [wave for *_, waves in parts for wave in waves]
    rows, width = adj.shape[0], 2 * arrays[0].shape[1]
    operands = [adj, *arrays] + ([] if start is None else [start])
    return in_vmem(functools.partial(gather_kernel, which), [kept((rows, width), dtype)], operands, name)[0]


def node_kernel(parts, base, degf_row, w_neigh, cotangent, grad, scaled_t, out):
    total = parts[0:TILE, :].astype(F32)
    for i in range(1, NCOL):
        total = total + parts[i * TILE : (i + 1) * TILE, :].astype(F32)
    degf_col = jnp.broadcast_to(degf_row[...], (TILE, TILE)).T[:, :1]
    mean = (total / degf_col).astype(BF16)
    pre = base[...] + jnp.dot(mean, w_neigh[...], preferred_element_type=F32)
    sig = jax.nn.sigmoid(pre)
    out[...] = (pre * sig).astype(BF16)
    slope = sig * (1.0 + pre * (1.0 - sig))
    grad_pre = (cotangent[...].astype(F32) * slope).astype(BF16)
    grad[...] = grad_pre
    proj_t = lax.dot_general(w_neigh[...], grad_pre, (((1,), (1,)), ((), ())), preferred_element_type=F32)
    scaled = (proj_t / degf_row[...]).astype(BF16)
    for i in range(NCOL):
        scaled_t[i, :, :] = scaled


def node_step(parts, base, degf_row, w_neigh, cotangent):
    rows, width = cotangent.shape
    results = [kept((rows, width), BF16), kept((NCOL, width, rows), BF16), plain((rows, width), BF16)]
    operands = (parts, base, degf_row, w_neigh, cotangent)
    return in_vmem(node_kernel, results, operands, "node_step", 4 * rows * width * width)


def spread_kernel(core, half, parts, adj, *outs):
    for w, out in enumerate(outs):
        rows = slice(0, SPLIT) if w == 0 else slice(SPLIT, parts.shape[1])
        lhs = jnp.concatenate([parts[i, rows, :] for i in range(NCOL)], axis=1)
        tiles = tiles_of(w, core, half)
        for i in range(0, len(tiles), NZH):
            rhs = columns(adj, slice(None), tiles[i : i + NZH])
            value = jnp.dot(lhs, rhs, preferred_element_type=F32)
            out[:, i * TILE : (i + NZH) * TILE] = value.astype(BF16)


def spread_matmul(parts, adj, core, half, name):
    cols = CHIPS // 2 * TILE
    results = [kept((rows, cols), BF16) for rows in (SPLIT, parts.shape[1] - SPLIT)]
    return in_vmem(functools.partial(spread_kernel, core, half), results, (parts, adj), name)


def sum_kernel(*refs):
    value = refs[0][...].astype(F32)
    for ref in refs[1:-1]:
        value = value + ref[...].astype(F32)
    refs[-1][...] = value.astype(BF16)


def pair_sum(mine, theirs):
    return in_vmem(sum_kernel, [kept(mine.shape, BF16)], (mine, theirs), "pair_sum")[0]


def split_kernel(*refs):
    value = refs[0][...].astype(F32)
    for ref in refs[1:-2]:
        value = value + ref[...].astype(F32)
    stay, go = refs[-2:]
    half = stay.shape[1]
    stay[...] = value[:, :half]
    go[...] = value[:, half:].astype(BF16)


def split_sum(values, name):
    rows, cols = values[0].shape
    results = [kept((rows, cols // 2), F32), kept((rows, cols // 2), BF16)]
    return in_vmem(split_kernel, results, values, name)


def last_kernel(*refs):
    waves, own, out = refs[:-2], refs[-2], refs[-1]
    back = [waves[i][...] + waves[i + 1][...].astype(F32) for i in range(0, len(waves), 2)]
    out[...] = (own[...] + jnp.concatenate(back, axis=0).T).astype(BF16)


def last_sum(waves, own):
    return in_vmem(last_kernel, [plain(own.shape, BF16)], (*waves, own), "last_sum")[0]


def body(features, degrees, tile_rows, tile_masks, w_self, w_neigh, bias, cotangent):
    row = lax.axis_index("row").astype(jnp.int32)

    device = jnp.arange(NROW, dtype=jnp.int32)
    differ = device ^ row
    bits = [(differ // (NZH * NCORE)) % NY, (differ // NCORE) % NZH]
    turn = []
    for d in bits:
        by_core = [jnp.where(d == k1, 1, jnp.where(d == k2, 2, jnp.where(d == 0, 0, 3))) for k1, k2 in STEPS]
        turn.append(jnp.where(device % NCORE == 0, *by_core))
    place = (differ % NCORE) * CHIPS + turn[0] * NZH + turn[1]
    adj = adjacency(tile_masks[0, 0], place.astype(jnp.int32), tile_rows[0, 0].reshape(-1))
    degf_row = degrees.astype(F32)[None, :]
    base = jnp.dot(features, w_self, preferred_element_type=F32) + bias[None, :]

    width = features.shape[1] // 2
    *got, adj = lax.optimization_barrier((*[exchange(features, a, 0) for a, _ in AXES], adj))
    waves = [join(features, g, w * width, width, "join_0") for w, g in enumerate(got)]
    got = [exchange(v, a, 1) for v, (a, _) in zip(waves, AXES)]
    waves = [join(v, g, 0, width, "join_1") for v, g in zip(waves, got)]
    got = [exchange(v, b, 0) for v, (_, b) in zip(waves, AXES)]
    got[1], base, degf_row = lax.optimization_barrier((got[1], base, degf_row))
    near = [join(v, g, 0, width, "join_2") for v, g in zip(waves, got)]
    far = [exchange(v, b, 1) for v, (_, b) in zip(near, AXES)]
    other = [swap(v) for v in near]
    part = gather_matmul(adj, [(0, 0, near), (1, 0, other)], None, F32, "gather_near")
    *far, part = lax.optimization_barrier((*far, part))
    other = [swap(v) for v in far]
    part = gather_matmul(adj, [(0, 1, far)], part, F32, "gather_far")
    *other, part = lax.optimization_barrier((*other, part))
    summed = gather_matmul(adj, [(1, 1, other)], part, BF16, "gather_far_other")

    arrived = lax.all_to_all(summed, "col", 0, 0, tiled=True)
    grad_pre, scaled_t, output = node_step(arrived, base, degf_row, w_neigh, cotangent)

    table = lax.all_to_all(scaled_t, "col", 0, 0, tiled=True)
    own = lax.dot_general(grad_pre, w_self, (((1,), (1,)), ((), ())), preferred_element_type=F32)

    theirs = [swap(v) for v in spread_matmul(table, adj, 1, 1, "spread_far_other")]
    mine = spread_matmul(table, adj, 0, 1, "spread_far")
    near_other = spread_matmul(table, adj, 1, 0, "spread_near_other")
    *theirs, table = lax.optimization_barrier((*theirs, *mine, *near_other, table))
    theirs, mine, near_other = theirs[:2], theirs[2:4], theirs[4:]
    values = [pair_sum(a, b) for a, b in zip(mine, theirs)]
    values[0], table = lax.optimization_barrier((values[0], table))
    got = [exchange(v, b, 1) for v, (_, b) in zip(values, AXES)]
    theirs = [swap(v) for v in near_other]
    mine = spread_matmul(table, adj, 0, 0, "spread_near")
    got[0], *mine = lax.optimization_barrier((got[0], *mine))
    ends = []
    for w, (a, b) in enumerate(AXES):
        stay, go = split_sum((mine[w], theirs[w], got[w]), "sum_3")
        stay, go = split_sum((stay, exchange(go, b, 0)), "sum_2")
        stay, go = split_sum((stay, exchange(go, a, 1)), "sum_1")
        ends += [stay, exchange(go, a, 0)]
    grad_features = last_sum(ends, own)
    return output, grad_features


def solution(mesh):
    both = P(("row", "col"), None)
    return jax.shard_map(
        body,
        mesh=mesh,
        in_specs=(
            both,
            P(("row", "col")),
            P("row", "col", None, None),
            P("row", "col", None, None, None, None),
            P(),
            P(),
            P(),
            both,
        ),
        out_specs=(both, both),
        check_vma=False,
    )
```

```python
import functools

import jax
import jax.numpy as jnp
from jax import lax
from jax.experimental import pallas as pl
from jax.experimental.pallas import tpu as pltpu
from jax.sharding import PartitionSpec as P

NY, NZH, NCORE, NX, NZL = 4, 4, 2, 4, 2
NROW, NCOL = NY * NZH * NCORE, NX * NZL
CHIPS = NY * NZH
STEPS = ((1, 3), (3, 1))
TILE = 128
AXES = (("z", "y"), ("y", "z"))
SPLIT = 320
BF16 = jnp.bfloat16
F32 = jnp.float32
MB = 1024 * 1024


def exchange(value, axis, step):
    pairs = []
    for row in range(NROW):
        bits = STEPS[row % NCORE][step]
        there = row ^ ((bits * NZH if axis == "y" else bits) * NCORE)
        pairs += [(row * NCOL + col, there * NCOL + col) for col in range(NCOL)]
    return lax.ppermute(value, ("row", "col"), pairs)


def swap(value):
    pairs = [(row * NCOL + col, (row ^ 1) * NCOL + col) for row in range(NROW) for col in range(NCOL)]
    return lax.ppermute(value, ("row", "col"), pairs)


def in_vmem(kernel, results, operands, name, flops=MB, grant=16, **extra):
    spec = pl.BlockSpec(memory_space=pltpu.VMEM)
    outs = [shape if plain else pltpu.VMEM(shape.shape, shape.dtype) for shape, plain in results]
    out_specs = [pl.BlockSpec() if plain else spec for _, plain in results]
    return pl.pallas_call(
        kernel,
        in_specs=[spec] * len(operands),
        out_specs=out_specs,
        out_shape=outs,
        compiler_params=pltpu.CompilerParams(vmem_limit_bytes=grant * MB),
        cost_estimate=pl.CostEstimate(flops=0, bytes_accessed=1024, transcendentals=0),
        name=name,
        **extra,
    )(*[pltpu.with_memory_space_constraint(v, pltpu.VMEM) for v in operands])


def kept(shape, dtype):
    return jax.ShapeDtypeStruct(shape, dtype), False


def plain(shape, dtype):
    return jax.ShapeDtypeStruct(shape, dtype), True


def adjacency_kernel(place, where, masks, out, held, sems):
    count, slots = masks.shape[0], masks.shape[1]
    copies = [pltpu.make_async_copy(masks.at[j], held.at[j], sems.at[j]) for j in range(count)]
    for copy in copies:
        copy.start()
    for j, copy in enumerate(copies):
        cols = pl.ds(pl.multiple_of(place[j] * TILE, TILE), TILE)
        out[:, cols] = jnp.zeros((out.shape[0], TILE), BF16)
        copy.wait()
        for k in range(slots):
            at = pl.ds(pl.multiple_of(where[j * slots + k] * TILE, TILE), TILE)
            out[at, cols] = out[at, cols] + held[j, k].astype(F32).astype(BF16)


def adjacency(masks, place, where):
    count = masks.shape[0]
    return pl.pallas_call(
        adjacency_kernel,
        grid_spec=pltpu.PrefetchScalarGridSpec(
            num_scalar_prefetch=2,
            grid=(1,),
            in_specs=[pl.BlockSpec(memory_space=pl.ANY)],
            out_specs=pl.BlockSpec(memory_space=pltpu.VMEM),
            scratch_shapes=[pltpu.VMEM(masks.shape, masks.dtype), pltpu.SemaphoreType.DMA((count,))],
        ),
        out_shape=pltpu.VMEM((NCOL * TILE, count * TILE), BF16),
        compiler_params=pltpu.CompilerParams(vmem_limit_bytes=16 * MB),
        cost_estimate=pl.CostEstimate(flops=0, bytes_accessed=14 * MB, transcendentals=0),
        name="adjacency",
    )(place, where, pltpu.with_memory_space_constraint(masks, pltpu.HBM))


def tiles_of(wave, core, half):
    out = []
    for n in range(half * CHIPS // 2, (half + 1) * CHIPS // 2):
        slow, fast = n // NZH, n % NZH
        out.append(core * CHIPS + (slow * NZH + fast if wave == 0 else fast * NZH + slow))
    return out


def columns(adj, rows, tiles):
    pieces = []
    for tile in tiles:
        if pieces and pieces[-1][1] == tile:
            pieces[-1][1] = tile + 1
        else:
            pieces.append([tile, tile + 1])
    parts = [adj[rows, a * TILE : b * TILE] for a, b in pieces]
    return parts[0] if len(parts) == 1 else jnp.concatenate(parts, axis=1)


def join_kernel(at, first, second, out):
    rows, width = first.shape[0], out.shape[1]
    out[:rows, :] = first[:, at : at + width]
    out[rows:, :] = second[:, at : at + width]


def join(first, second, at, width, name):
    shape = (2 * first.shape[0], width)
    return in_vmem(functools.partial(join_kernel, at), [kept(shape, BF16)], (first, second), name)[0]


def gather_kernel(parts, adj, *refs):
    out = refs[-1]
    start = refs[-2] if len(refs) > 2 * len(parts) + 1 else None
    width = out.shape[1] // 2
    step = 2 * TILE
    for w in range(2):
        cols = slice(w * width, (w + 1) * width)
        rhs = jnp.concatenate([refs[2 * i + w][...] for i in range(len(parts))], axis=0)
        tiles = [tile for core, half in parts for tile in tiles_of(w, core, half)]
        for r in range(0, out.shape[0], step):
            rows = slice(r, r + step)
            value = jnp.dot(columns(adj, rows, tiles), rhs, preferred_element_type=F32)
            if start is not None:
                value = value + start[rows, cols]
            out[rows, cols] = value.astype(out.dtype)


def gather_matmul(adj, parts, start, dtype, name):
    which = [(core, half) for core, half, _ in parts]
    arrays = [wave for *_, waves in parts for wave in waves]
    rows, width = adj.shape[0], 2 * arrays[0].shape[1]
    operands = [adj, *arrays] + ([] if start is None else [start])
    return in_vmem(functools.partial(gather_kernel, which), [kept((rows, width), dtype)], operands, name)[0]


def node_kernel(parts, base, degf_row, w_neigh, cotangent, grad, scaled_t, out):
    total = parts[0:TILE, :].astype(F32)
    for i in range(1, NCOL):
        total = total + parts[i * TILE : (i + 1) * TILE, :].astype(F32)
    degf_col = jnp.broadcast_to(degf_row[...], (TILE, TILE)).T[:, :1]
    mean = (total / degf_col).astype(BF16)
    pre = base[...] + jnp.dot(mean, w_neigh[...], preferred_element_type=F32)
    sig = jax.nn.sigmoid(pre)
    out[...] = (pre * sig).astype(BF16)
    slope = sig * (1.0 + pre * (1.0 - sig))
    grad_pre = (cotangent[...].astype(F32) * slope).astype(BF16)
    grad[...] = grad_pre
    proj_t = lax.dot_general(w_neigh[...], grad_pre, (((1,), (1,)), ((), ())), preferred_element_type=F32)
    scaled = (proj_t / degf_row[...]).astype(BF16)
    for i in range(NCOL):
        scaled_t[i, :, :] = scaled


def node_step(parts, base, degf_row, w_neigh, cotangent):
    rows, width = cotangent.shape
    results = [kept((rows, width), BF16), kept((NCOL, width, rows), BF16), plain((rows, width), BF16)]
    operands = (parts, base, degf_row, w_neigh, cotangent)
    return in_vmem(node_kernel, results, operands, "node_step", 4 * rows * width * width)


def spread_kernel(core, half, parts, adj, *outs):
    for w, out in enumerate(outs):
        rows = slice(0, SPLIT) if w == 0 else slice(SPLIT, parts.shape[1])
        lhs = jnp.concatenate([parts[i, rows, :] for i in range(NCOL)], axis=1)
        tiles = tiles_of(w, core, half)
        for i in range(0, len(tiles), NZH):
            rhs = columns(adj, slice(None), tiles[i : i + NZH])
            value = jnp.dot(lhs, rhs, preferred_element_type=F32)
            out[:, i * TILE : (i + NZH) * TILE] = value.astype(BF16)


def spread_matmul(parts, adj, core, half, name):
    cols = CHIPS // 2 * TILE
    results = [kept((rows, cols), BF16) for rows in (SPLIT, parts.shape[1] - SPLIT)]
    return in_vmem(functools.partial(spread_kernel, core, half), results, (parts, adj), name)


def sum_kernel(*refs):
    value = refs[0][...].astype(F32)
    for ref in refs[1:-1]:
        value = value + ref[...].astype(F32)
    refs[-1][...] = value.astype(BF16)


def pair_sum(mine, theirs):
    return in_vmem(sum_kernel, [kept(mine.shape, BF16)], (mine, theirs), "pair_sum")[0]


def split_kernel(*refs):
    value = refs[0][...].astype(F32)
    for ref in refs[1:-2]:
        value = value + ref[...].astype(F32)
    stay, go = refs[-2:]
    half = stay.shape[1]
    stay[...] = value[:, :half]
    go[...] = value[:, half:].astype(BF16)


def split_sum(values, name):
    rows, cols = values[0].shape
    results = [kept((rows, cols // 2), F32), kept((rows, cols // 2), BF16)]
    return in_vmem(split_kernel, results, values, name)


def last_kernel(*refs):
    waves, own, out = refs[:-2], refs[-2], refs[-1]
    back = [waves[i][...] + waves[i + 1][...].astype(F32) for i in range(0, len(waves), 2)]
    out[...] = (own[...] + jnp.concatenate(back, axis=0).T).astype(BF16)


def last_sum(waves, own):
    return in_vmem(last_kernel, [plain(own.shape, BF16)], (*waves, own), "last_sum")[0]


def body(features, degrees, tile_rows, tile_masks, w_self, w_neigh, bias, cotangent):
    row = lax.axis_index("row").astype(jnp.int32)

    device = jnp.arange(NROW, dtype=jnp.int32)
    differ = device ^ row
    bits = [(differ // (NZH * NCORE)) % NY, (differ // NCORE) % NZH]
    turn = []
    for d in bits:
        by_core = [jnp.where(d == k1, 1, jnp.where(d == k2, 2, jnp.where(d == 0, 0, 3))) for k1, k2 in STEPS]
        turn.append(jnp.where(device % NCORE == 0, *by_core))
    place = (differ % NCORE) * CHIPS + turn[0] * NZH + turn[1]
    adj = adjacency(tile_masks[0, 0], place.astype(jnp.int32), tile_rows[0, 0].reshape(-1))
    degf_row = degrees.astype(F32)[None, :]
    base = jnp.dot(features, w_self, preferred_element_type=F32) + bias[None, :]

    width = features.shape[1] // 2
    got = [exchange(features, a, 0) for a, _ in AXES]
    waves = [join(features, g, w * width, width, "join_0") for w, g in enumerate(got)]
    got = [exchange(v, a, 1) for v, (a, _) in zip(waves, AXES)]
    got[1], base, degf_row = lax.optimization_barrier((got[1], base, degf_row))
    waves = [join(v, g, 0, width, "join_1") for v, g in zip(waves, got)]
    got = [exchange(v, b, 0) for v, (_, b) in zip(waves, AXES)]
    near = [join(v, g, 0, width, "join_2") for v, g in zip(waves, got)]
    far = [exchange(v, b, 1) for v, (_, b) in zip(near, AXES)]
    other = [swap(v) for v in near]
    part = gather_matmul(adj, [(0, 0, near), (1, 0, other)], None, F32, "gather_near")
    *far, part = lax.optimization_barrier((*far, part))
    other = [swap(v) for v in far]
    part = gather_matmul(adj, [(0, 1, far)], part, F32, "gather_far")
    *other, part = lax.optimization_barrier((*other, part))
    summed = gather_matmul(adj, [(1, 1, other)], part, BF16, "gather_far_other")

    arrived = lax.all_to_all(summed, "col", 0, 0, tiled=True)
    grad_pre, scaled_t, output = node_step(arrived, base, degf_row, w_neigh, cotangent)

    table = lax.all_to_all(scaled_t, "col", 0, 0, tiled=True)
    own = lax.dot_general(grad_pre, w_self, (((1,), (1,)), ((), ())), preferred_element_type=F32)

    theirs = [swap(v) for v in spread_matmul(table, adj, 1, 1, "spread_far_other")]
    mine = spread_matmul(table, adj, 0, 1, "spread_far")
    near_other = spread_matmul(table, adj, 1, 0, "spread_near_other")
    *theirs, table = lax.optimization_barrier((*theirs, *mine, *near_other, table))
    theirs, mine, near_other = theirs[:2], theirs[2:4], theirs[4:]
    values = [pair_sum(a, b) for a, b in zip(mine, theirs)]
    values[0], table = lax.optimization_barrier((values[0], table))
    got = [exchange(v, b, 1) for v, (_, b) in zip(values, AXES)]
    theirs = [swap(v) for v in near_other]
    mine = spread_matmul(table, adj, 0, 0, "spread_near")
    got[0], *mine = lax.optimization_barrier((got[0], *mine))
    stay, go = [None, None], [None, None]
    for step in range(3):
        for w, (a, b) in enumerate(AXES):
            if w == 1 and step == 2:
                got[1], go[0] = lax.optimization_barrier((got[1], go[0]))
            terms = (mine[w], theirs[w], got[w]) if step == 0 else (stay[w], got[w])
            stay[w], go[w] = split_sum(terms, f"sum_{step}")
        got = [exchange(v, axes[1 - (step + 1) // 2], (step + 1) % 2 ^ 1) for v, axes in zip(go, AXES)]
    ends = [stay[0], got[0], stay[1], got[1]]
    grad_features = last_sum(ends, own)
    return output, grad_features


def solution(mesh):
    both = P(("row", "col"), None)
    return jax.shard_map(
        body,
        mesh=mesh,
        in_specs=(
            both,
            P(("row", "col")),
            P("row", "col", None, None),
            P("row", "col", None, None, None, None),
            P(),
            P(),
            P(),
            both,
        ),
        out_specs=(both, both),
        check_vma=False,
    )
```

```python
import functools

import jax
import jax.numpy as jnp
from jax import lax
from jax.experimental import pallas as pl
from jax.experimental.pallas import tpu as pltpu
from jax.sharding import PartitionSpec as P

NY, NZH, NCORE, NX, NZL = 4, 4, 2, 4, 2
NROW, NCOL = NY * NZH * NCORE, NX * NZL
CHIPS = NY * NZH
STEPS = ((1, 3), (3, 1))
TILE = 128
BF16 = jnp.bfloat16
F32 = jnp.float32
MB = 1024 * 1024


def flip(value, y=0, z=0, core=0):
    pairs = []
    for row in range(NROW):
        there = row ^ ((y * NZH + z) * NCORE + core)
        pairs += [(row * NCOL + col, there * NCOL + col) for col in range(NCOL)]
    return lax.ppermute(value, ("row", "col"), pairs)


def in_vmem(kernel, results, operands, name, flops=MB, grant=8, **extra):
    spec = pl.BlockSpec(memory_space=pltpu.VMEM)
    outs = [shape if plain else pltpu.VMEM(shape.shape, shape.dtype) for shape, plain in results]
    out_specs = [pl.BlockSpec() if plain else spec for _, plain in results]
    return pl.pallas_call(
        kernel,
        in_specs=[spec] * len(operands),
        out_specs=out_specs,
        out_shape=outs,
        compiler_params=pltpu.CompilerParams(vmem_limit_bytes=grant * MB),
        cost_estimate=pl.CostEstimate(flops=flops, bytes_accessed=3 * MB, transcendentals=0),
        name=name,
        **extra,
    )(*[pltpu.with_memory_space_constraint(v, pltpu.VMEM) for v in operands])


def kept(shape, dtype):
    return jax.ShapeDtypeStruct(shape, dtype), False


def plain(shape, dtype):
    return jax.ShapeDtypeStruct(shape, dtype), True


def adjacency_kernel(place, where, masks, out, held, sems):
    count, slots = masks.shape[0], masks.shape[1]
    copies = [pltpu.make_async_copy(masks.at[j], held.at[j], sems.at[j]) for j in range(count)]
    for copy in copies:
        copy.start()
    for j, copy in enumerate(copies):
        cols = pl.ds(pl.multiple_of(place[j] * TILE, TILE), TILE)
        out[:, cols] = jnp.zeros((out.shape[0], TILE), BF16)
        copy.wait()
        for k in range(slots):
            at = pl.ds(pl.multiple_of(where[j * slots + k] * TILE, TILE), TILE)
            out[at, cols] = out[at, cols] + held[j, k].astype(F32).astype(BF16)


def adjacency(masks, place, where):
    count = masks.shape[0]
    return pl.pallas_call(
        adjacency_kernel,
        grid_spec=pltpu.PrefetchScalarGridSpec(
            num_scalar_prefetch=2,
            grid=(1,),
            in_specs=[pl.BlockSpec(memory_space=pl.ANY)],
            out_specs=pl.BlockSpec(memory_space=pltpu.VMEM),
            scratch_shapes=[pltpu.VMEM(masks.shape, masks.dtype), pltpu.SemaphoreType.DMA((count,))],
        ),
        out_shape=pltpu.VMEM((NCOL * TILE, count * TILE), BF16),
        compiler_params=pltpu.CompilerParams(vmem_limit_bytes=8 * MB),
        cost_estimate=pl.CostEstimate(flops=0, bytes_accessed=14 * MB, transcendentals=0),
        name="adjacency",
    )(place, where, pltpu.with_memory_space_constraint(masks, pltpu.HBM))


def gather_kernel(cores, dys, adj, *refs):
    parts, out = refs[: 2 * len(cores)], refs[-1]
    start = refs[-2] if len(refs) > len(parts) + 1 else None
    half = parts[0].shape[1]
    depth = NZH * TILE
    rows = 2 * TILE
    for r in range(0, out.shape[0], rows):
        for h in range(2):
            cols = slice(h * half, (h + 1) * half)
            value = None if start is None else start[r : r + rows, cols]
            for i, core in enumerate(cores):
                at = [(core * NY + dy) * depth for dy in dys[h]]
                lhs = jnp.concatenate([adj[r : r + rows, a : a + depth] for a in at], axis=1)
                term = jnp.dot(lhs, parts[2 * i + h][...], preferred_element_type=F32)
                value = term if value is None else value + term
            out[r : r + rows, cols] = value.astype(out.dtype)


def gather_matmul(adj, parts, cores, dys, start, dtype, name):
    rows, width = adj.shape[0], 2 * parts[0].shape[1]
    operands = [adj, *parts] + ([] if start is None else [start])
    flops = 2 * rows * width * parts[0].shape[0] * len(cores)
    return in_vmem(functools.partial(gather_kernel, cores, dys), [kept((rows, width), dtype)], operands, name, flops)[0]


def node_kernel(parts, base, degf_row, w_neigh, cotangent, grad, scaled_t, out):
    total = parts[0:TILE, :].astype(F32)
    for i in range(1, NCOL):
        total = total + parts[i * TILE : (i + 1) * TILE, :].astype(F32)
    degf_col = jnp.broadcast_to(degf_row[...], (TILE, TILE)).T[:, :1]
    mean = (total / degf_col).astype(BF16)
    pre = base[...] + jnp.dot(mean, w_neigh[...], preferred_element_type=F32)
    sig = jax.nn.sigmoid(pre)
    out[...] = (pre * sig).astype(BF16)
    slope = sig * (1.0 + pre * (1.0 - sig))
    grad_pre = (cotangent[...].astype(F32) * slope).astype(BF16)
    grad[...] = grad_pre
    proj_t = lax.dot_general(w_neigh[...], grad_pre, (((1,), (1,)), ((), ())), preferred_element_type=F32)
    scaled = (proj_t / degf_row[...]).astype(BF16)
    for i in range(NCOL):
        scaled_t[i, :, :] = scaled


def node_step(parts, base, degf_row, w_neigh, cotangent):
    rows, width = cotangent.shape
    results = [kept((rows, width), BF16), kept((NCOL, width, rows), BF16), plain((rows, width), BF16)]
    operands = (parts, base, degf_row, w_neigh, cotangent)
    return in_vmem(node_kernel, results, operands, "node_step", 4 * rows * width * width)


def spread_kernel(core, pick, parts, adj, out):
    depth = NZH * TILE
    half = out.shape[1]
    for h, steps in enumerate(STEPS):
        lhs = jnp.concatenate([parts[i, h * half : (h + 1) * half, :] for i in range(NCOL)], axis=1)
        for n, dy in enumerate(pick(*steps)):
            at = (core * NY + dy) * depth
            value = jnp.dot(lhs, adj[:, at : at + depth], preferred_element_type=F32)
            out[h, :, n * depth : (n + 1) * depth] = value.astype(BF16)


def spread_matmul(parts, adj, core, pick, name):
    shape = (2, parts.shape[1] // 2, 2 * NZH * TILE)
    return in_vmem(functools.partial(spread_kernel, core, pick), [kept(shape, BF16)], (parts, adj), name)[0]


def goes(k1, k2):
    return k2, k1 ^ k2


def stays(k1, k2):
    return 0, k1


def total(refs):
    value = refs[0][...].astype(F32)
    for ref in refs[1:]:
        value = value + ref[...].astype(F32)
    return value


def both_halves_kernel(mine, theirs, *outs):
    for h, out in enumerate(outs):
        out[...] = (mine[h].astype(F32) + theirs[h].astype(F32)).astype(BF16)


def both_halves(mine, theirs):
    return in_vmem(both_halves_kernel, [kept(mine.shape[1:], BF16)] * 2, (mine, theirs), "both_halves")


def first_split_kernel(h, mine, theirs, got, stay, go):
    value = mine[h].astype(F32) + theirs[h].astype(F32) + got[...].astype(F32)
    depth = stay.shape[1]
    stay[...] = value[:, :depth]
    go[...] = value[:, depth:].astype(BF16)


def first_split(h, mine, theirs, got, name):
    shape = (got.shape[0], got.shape[1] // 2)
    results = [kept(shape, F32), kept(shape, BF16)]
    return in_vmem(functools.partial(first_split_kernel, h), results, (mine, theirs, got), name)


def split_kernel(stays, goes, *refs):
    value = total(refs[:-2])
    for out, tiles in zip(refs[-2:], (stays, goes)):
        for i, tile in enumerate(tiles):
            part = value[:, tile * TILE : (tile + 1) * TILE]
            out[:, i * TILE : (i + 1) * TILE] = part.astype(out.dtype)


def add_split(values, stays, goes, name):
    rows = values[0].shape[0]
    results = [kept((rows, len(stays) * TILE), F32), kept((rows, len(goes) * TILE), BF16)]
    return in_vmem(functools.partial(split_kernel, stays, goes), results, values, name)


def last_kernel(*refs):
    own, out = refs[-2:]
    back = jnp.concatenate([total(refs[0:2]), total(refs[2:4])], axis=0)
    out[...] = (own[...] + back.T).astype(BF16)


def last_sum(values, own):
    return in_vmem(last_kernel, [plain(own.shape, BF16)], (*values, own), "last_sum")[0]


def body(features, degrees, tile_rows, tile_masks, w_self, w_neigh, bias, cotangent):
    half = features.shape[1] // 2
    row = lax.axis_index("row").astype(jnp.int32)

    differ = jnp.arange(NROW, dtype=jnp.int32) ^ row
    adj = adjacency(tile_masks[0, 0], (differ % NCORE) * CHIPS + differ // NCORE, tile_rows[0, 0].reshape(-1))
    degf_row = degrees.astype(F32)[None, :]
    base = jnp.dot(features, w_self, preferred_element_type=F32) + bias[None, :]

    chunks = [features[:, :half], features[:, half:]]
    firsts = [flip(v, z=k1) for v, (k1, _) in zip(chunks, STEPS)]
    pairs = [jnp.concatenate([v, r], axis=0) for v, r in zip(chunks, firsts)]
    seconds = [flip(v, z=k2) for v, (_, k2) in zip(pairs, STEPS)]
    planes = []
    for v, first, second, (k1, k2) in zip(chunks, firsts, seconds, STEPS):
        tiles = {0: v, k1: first, k2: second[:TILE], k1 ^ k2: second[TILE:]}
        planes.append(jnp.concatenate([tiles[i] for i in range(NZH)], axis=0))
    thirds = [flip(v, y=k1) for v, (k1, _) in zip(planes, STEPS)]
    *thirds, adj, base, degf_row = lax.optimization_barrier((*thirds, adj, base, degf_row))
    near = [jnp.concatenate([v, r], axis=0) for v, r in zip(planes, thirds)]
    far = [flip(v, y=k2) for v, (_, k2) in zip(near, STEPS)]
    first, second = [(0, k1) for k1, _ in STEPS], [(k2, k1 ^ k2) for k1, k2 in STEPS]
    near = near + [flip(v, core=1) for v in near]
    part = gather_matmul(adj, near, (0, 1), first, None, F32, "gather_near")
    far[0], part = lax.optimization_barrier((far[0], part))
    other = [flip(v, core=1) for v in far]
    part = gather_matmul(adj, far, (0,), second, part, F32, "gather_far")
    *other, part = lax.optimization_barrier((*other, part))
    summed = gather_matmul(adj, other, (1,), second, part, BF16, "gather_far_other")

    arrived = lax.all_to_all(summed, "col", 0, 0, tiled=True)
    grad_pre, scaled_t, output = node_step(arrived, base, degf_row, w_neigh, cotangent)

    table = lax.all_to_all(scaled_t, "col", 0, 0, tiled=True)
    own = lax.dot_general(grad_pre, w_self, (((1,), (1,)), ((), ())), preferred_element_type=F32)
    send_in = flip(spread_matmul(table, adj, 1, goes, "spread_go_other"), core=1)
    send = spread_matmul(table, adj, 0, goes, "spread_go")
    keep_out = spread_matmul(table, adj, 1, stays, "spread_stay_other")
    send_in, send, keep_out = lax.optimization_barrier((send_in, send, keep_out))
    sums = list(both_halves(send, send_in))
    sums[0], table = lax.optimization_barrier((sums[0], table))
    keep_in = flip(keep_out, core=1)
    keep = spread_matmul(table, adj, 0, stays, "spread_stay")

    ends = []
    for h, (value, (k1, k2)) in enumerate(zip(sums, STEPS)):
        got = flip(value, y=k2)
        stay, go = first_split(h, keep, keep_in, got, "add_y1")
        got = flip(go, y=k1)
        stay, go = add_split((stay, got), (0, k1), (k2, k1 ^ k2), "add_y2")
        got = flip(go, z=k2)
        stay, go = add_split((stay, got), (0,), (1,), "add_z1")
        ends += [stay, flip(go, z=k1)]
    grad_features = last_sum(ends, own)
    return output, grad_features


def solution(mesh):
    both = P(("row", "col"), None)
    return jax.shard_map(
        body,
        mesh=mesh,
        in_specs=(
            both,
            P(("row", "col")),
            P("row", "col", None, None),
            P("row", "col", None, None, None, None),
            P(),
            P(),
            P(),
            both,
        ),
        out_specs=(both, both),
        check_vma=False,
    )
```

```python
import functools

import jax
import jax.numpy as jnp
from jax import lax
from jax.experimental import pallas as pl
from jax.experimental.pallas import tpu as pltpu
from jax.sharding import PartitionSpec as P

NY, NZH, NCORE, NX, NZL = 4, 4, 2, 4, 2
NROW, NCOL = NY * NZH * NCORE, NX * NZL
CHIPS = NY * NZH
STEPS = ((1, 3), (3, 1))
TILE = 128
BF16 = jnp.bfloat16
F32 = jnp.float32
MB = 1024 * 1024


def flip(value, y=0, z=0, core=0):
    pairs = []
    for row in range(NROW):
        there = row ^ ((y * NZH + z) * NCORE + core)
        pairs += [(row * NCOL + col, there * NCOL + col) for col in range(NCOL)]
    return lax.ppermute(value, ("row", "col"), pairs)


def in_vmem(kernel, results, operands, name, flops=MB, grant=8, **extra):
    spec = pl.BlockSpec(memory_space=pltpu.VMEM)
    outs = [shape if plain else pltpu.VMEM(shape.shape, shape.dtype) for shape, plain in results]
    out_specs = [pl.BlockSpec() if plain else spec for _, plain in results]
    return pl.pallas_call(
        kernel,
        in_specs=[spec] * len(operands),
        out_specs=out_specs,
        out_shape=outs,
        compiler_params=pltpu.CompilerParams(vmem_limit_bytes=grant * MB),
        cost_estimate=pl.CostEstimate(flops=flops, bytes_accessed=3 * MB, transcendentals=0),
        name=name,
        **extra,
    )(*[pltpu.with_memory_space_constraint(v, pltpu.VMEM) for v in operands])


def kept(shape, dtype):
    return jax.ShapeDtypeStruct(shape, dtype), False


def plain(shape, dtype):
    return jax.ShapeDtypeStruct(shape, dtype), True


def adjacency_kernel(place, where, masks, out, held, sems):
    count, slots = masks.shape[0], masks.shape[1]
    copies = [pltpu.make_async_copy(masks.at[j], held.at[j], sems.at[j]) for j in range(count)]
    for copy in copies:
        copy.start()
    for j, copy in enumerate(copies):
        cols = pl.ds(pl.multiple_of(place[j] * TILE, TILE), TILE)
        out[:, cols] = jnp.zeros((out.shape[0], TILE), BF16)
        copy.wait()
        for k in range(slots):
            at = pl.ds(pl.multiple_of(where[j * slots + k] * TILE, TILE), TILE)
            out[at, cols] = out[at, cols] + held[j, k].astype(F32).astype(BF16)


def adjacency(masks, place, where):
    count = masks.shape[0]
    return pl.pallas_call(
        adjacency_kernel,
        grid_spec=pltpu.PrefetchScalarGridSpec(
            num_scalar_prefetch=2,
            grid=(1,),
            in_specs=[pl.BlockSpec(memory_space=pl.ANY)],
            out_specs=pl.BlockSpec(memory_space=pltpu.VMEM),
            scratch_shapes=[pltpu.VMEM(masks.shape, masks.dtype), pltpu.SemaphoreType.DMA((count,))],
        ),
        out_shape=pltpu.VMEM((NCOL * TILE, count * TILE), BF16),
        compiler_params=pltpu.CompilerParams(vmem_limit_bytes=8 * MB),
        cost_estimate=pl.CostEstimate(flops=0, bytes_accessed=14 * MB, transcendentals=0),
        name="adjacency",
    )(place, where, pltpu.with_memory_space_constraint(masks, pltpu.HBM))


def gather_kernel(cores, dys, halves, adj, *refs):
    parts, start, out = refs[: len(halves) * len(cores)], None, refs[-1]
    if len(refs) > len(parts) + 1:
        start = refs[-2]
    half = parts[0].shape[1]
    depth = NZH * TILE
    rows = 2 * TILE
    for r in range(0, out.shape[0], rows):
        for n, h in enumerate(halves):
            cols = slice(h * half, (h + 1) * half)
            value = None if start is None else start[r : r + rows, cols].astype(F32)
            for i, core in enumerate(cores):
                at = [(core * NY + dy) * depth for dy in dys[h]]
                lhs = jnp.concatenate([adj[r : r + rows, a : a + depth] for a in at], axis=1)
                term = jnp.dot(lhs, parts[len(halves) * i + n][...], preferred_element_type=F32)
                value = term if value is None else value + term
            out[r : r + rows, cols] = value.astype(out.dtype)
        for h in set(range(2)) - set(halves):
            cols = slice(h * half, (h + 1) * half)
            out[r : r + rows, cols] = start[r : r + rows, cols].astype(out.dtype)


def gather_matmul(adj, parts, cores, dys, start, dtype, name, halves=(0, 1)):
    rows, width = adj.shape[0], 2 * parts[0].shape[1]
    operands = [adj, *parts] + ([] if start is None else [start])
    kernel = functools.partial(gather_kernel, cores, dys, halves)
    return in_vmem(kernel, [kept((rows, width), dtype)], operands, name)[0]


def node_kernel(parts, base, degf_row, w_neigh, cotangent, grad, scaled_t, out):
    total = parts[0:TILE, :].astype(F32)
    for i in range(1, NCOL):
        total = total + parts[i * TILE : (i + 1) * TILE, :].astype(F32)
    degf_col = jnp.broadcast_to(degf_row[...], (TILE, TILE)).T[:, :1]
    mean = (total / degf_col).astype(BF16)
    pre = base[...] + jnp.dot(mean, w_neigh[...], preferred_element_type=F32)
    sig = jax.nn.sigmoid(pre)
    out[...] = (pre * sig).astype(BF16)
    slope = sig * (1.0 + pre * (1.0 - sig))
    grad_pre = (cotangent[...].astype(F32) * slope).astype(BF16)
    grad[...] = grad_pre
    proj_t = lax.dot_general(w_neigh[...], grad_pre, (((1,), (1,)), ((), ())), preferred_element_type=F32)
    scaled = (proj_t / degf_row[...]).astype(BF16)
    for i in range(NCOL):
        scaled_t[i, :, :] = scaled


def node_step(parts, base, degf_row, w_neigh, cotangent):
    rows, width = cotangent.shape
    results = [kept((rows, width), BF16), kept((NCOL, width, rows), BF16), plain((rows, width), BF16)]
    operands = (parts, base, degf_row, w_neigh, cotangent)
    return in_vmem(node_kernel, results, operands, "node_step", 4 * rows * width * width)


def spread_kernel(core, pick, parts, adj, out):
    depth = NZH * TILE
    half = out.shape[1]
    for h, steps in enumerate(STEPS):
        lhs = jnp.concatenate([parts[i, h * half : (h + 1) * half, :] for i in range(NCOL)], axis=1)
        for n, dy in enumerate(pick(*steps)):
            at = (core * NY + dy) * depth
            value = jnp.dot(lhs, adj[:, at : at + depth], preferred_element_type=F32)
            out[h, :, n * depth : (n + 1) * depth] = value.astype(BF16)


def spread_matmul(parts, adj, core, pick, name):
    shape = (2, parts.shape[1] // 2, 2 * NZH * TILE)
    return in_vmem(functools.partial(spread_kernel, core, pick), [kept(shape, BF16)], (parts, adj), name)[0]


def goes(k1, k2):
    return k2, k1 ^ k2


def stays(k1, k2):
    return 0, k1


def total(refs):
    value = refs[0][...].astype(F32)
    for ref in refs[1:]:
        value = value + ref[...].astype(F32)
    return value


def both_halves_kernel(mine, theirs, *outs):
    for h, out in enumerate(outs):
        out[...] = (mine[h].astype(F32) + theirs[h].astype(F32)).astype(BF16)


def both_halves(mine, theirs):
    return in_vmem(both_halves_kernel, [kept(mine.shape[1:], BF16)] * 2, (mine, theirs), "both_halves")


def first_split_kernel(h, mine, theirs, got, stay, go):
    value = mine[h].astype(F32) + theirs[h].astype(F32) + got[...].astype(F32)
    depth = stay.shape[1]
    stay[...] = value[:, :depth]
    go[...] = value[:, depth:].astype(BF16)


def first_split(h, mine, theirs, got, name):
    shape = (got.shape[0], got.shape[1] // 2)
    results = [kept(shape, F32), kept(shape, BF16)]
    return in_vmem(functools.partial(first_split_kernel, h), results, (mine, theirs, got), name)


def split_kernel(stays, goes, *refs):
    value = total(refs[:-2])
    for out, tiles in zip(refs[-2:], (stays, goes)):
        for i, tile in enumerate(tiles):
            part = value[:, tile * TILE : (tile + 1) * TILE]
            out[:, i * TILE : (i + 1) * TILE] = part.astype(out.dtype)


def add_split(values, stays, goes, name):
    rows = values[0].shape[0]
    results = [kept((rows, len(stays) * TILE), F32), kept((rows, len(goes) * TILE), BF16)]
    return in_vmem(functools.partial(split_kernel, stays, goes), results, values, name)


def last_kernel(*refs):
    own, out = refs[-2:]
    back = jnp.concatenate([total(refs[0:2]), total(refs[2:4])], axis=0)
    out[...] = (own[...] + back.T).astype(BF16)


def last_sum(values, own):
    return in_vmem(last_kernel, [plain(own.shape, BF16)], (*values, own), "last_sum")[0]


def body(features, degrees, tile_rows, tile_masks, w_self, w_neigh, bias, cotangent):
    half = features.shape[1] // 2
    row = lax.axis_index("row").astype(jnp.int32)

    differ = jnp.arange(NROW, dtype=jnp.int32) ^ row
    place = (differ % NCORE) * CHIPS + differ // NCORE
    where = tile_rows[0, 0].reshape(-1)
    degf_row = degrees.astype(F32)[None, :]
    base = jnp.dot(features, w_self, preferred_element_type=F32) + bias[None, :]

    chunks = [features[:, :half], features[:, half:]]
    firsts = [flip(v, z=k1) for v, (k1, _) in zip(chunks, STEPS)]
    pairs = [jnp.concatenate([v, r], axis=0) for v, r in zip(chunks, firsts)]
    seconds = [flip(v, z=k2) for v, (_, k2) in zip(pairs, STEPS)]
    seconds[0], place, where, degf_row = lax.optimization_barrier((seconds[0], place, where, degf_row))
    adj = adjacency(tile_masks[0, 0], place, where)
    planes = []
    for v, first, second, (k1, k2) in zip(chunks, firsts, seconds, STEPS):
        tiles = {0: v, k1: first, k2: second[:TILE], k1 ^ k2: second[TILE:]}
        planes.append(jnp.concatenate([tiles[i] for i in range(NZH)], axis=0))
    thirds = [flip(v, y=k1) for v, (k1, _) in zip(planes, STEPS)]
    *thirds, adj, base = lax.optimization_barrier((*thirds, adj, base))
    near = [jnp.concatenate([v, r], axis=0) for v, r in zip(planes, thirds)]
    far = [flip(v, y=k2) for v, (_, k2) in zip(near, STEPS)]
    first, second = [(0, k1) for k1, _ in STEPS], [(k2, k1 ^ k2) for k1, k2 in STEPS]
    near = near + [flip(v, core=1) for v in near]
    part = gather_matmul(adj, near, (0, 1), first, None, F32, "gather_near")
    far[0], part = lax.optimization_barrier((far[0], part))
    other = [flip(v, core=1) for v in far]
    part = gather_matmul(adj, far, (0,), second, part, F32, "gather_far")
    other[0], part = lax.optimization_barrier((other[0], part))
    part = gather_matmul(adj, other[:1], (1,), second, part, F32, "gather_far_first", (0,))
    other[1], part = lax.optimization_barrier((other[1], part))
    summed = gather_matmul(adj, other[1:], (1,), second, part, BF16, "gather_far_second", (1,))

    arrived = lax.all_to_all(summed, "col", 0, 0, tiled=True)
    grad_pre, scaled_t, output = node_step(arrived, base, degf_row, w_neigh, cotangent)

    table = lax.all_to_all(scaled_t, "col", 0, 0, tiled=True)
    own = lax.dot_general(grad_pre, w_self, (((1,), (1,)), ((), ())), preferred_element_type=F32)
    send_in = flip(spread_matmul(table, adj, 1, goes, "spread_go_other"), core=1)
    send = spread_matmul(table, adj, 0, goes, "spread_go")
    keep_out = spread_matmul(table, adj, 1, stays, "spread_stay_other")
    send_in, send, keep_out = lax.optimization_barrier((send_in, send, keep_out))
    sums = list(both_halves(send, send_in))
    sums[0], keep_out, table = lax.optimization_barrier((sums[0], keep_out, table))
    keep_in = flip(keep_out, core=1)
    keep = spread_matmul(table, adj, 0, stays, "spread_stay")

    ends = []
    for h, (value, (k1, k2)) in enumerate(zip(sums, STEPS)):
        got = flip(value, y=k2)
        stay, go = first_split(h, keep, keep_in, got, "add_y1")
        got = flip(go, y=k1)
        stay, go = add_split((stay, got), (0, k1), (k2, k1 ^ k2), "add_y2")
        got = flip(go, z=k2)
        stay, go = add_split((stay, got), (0,), (1,), "add_z1")
        ends += [stay, flip(go, z=k1)]
    grad_features = last_sum(ends, own)
    return output, grad_features


def solution(mesh):
    both = P(("row", "col"), None)
    return jax.shard_map(
        body,
        mesh=mesh,
        in_specs=(
            both,
            P(("row", "col")),
            P("row", "col", None, None),
            P("row", "col", None, None, None, None),
            P(),
            P(),
            P(),
            both,
        ),
        out_specs=(both, both),
        check_vma=False,
    )
```

```python
import functools

import jax
import jax.numpy as jnp
from jax import lax
from jax.experimental import pallas as pl
from jax.experimental.pallas import tpu as pltpu
from jax.sharding import PartitionSpec as P

NY, NZH, NCORE, NX, NZL = 4, 4, 2, 4, 2
NROW, NCOL = NY * NZH * NCORE, NX * NZL
CHIPS = NY * NZH
STEPS = ((1, 3), (3, 1))
TILE = 128
BF16 = jnp.bfloat16
F32 = jnp.float32
MB = 1024 * 1024


def flip(value, y=0, z=0, core=0):
    pairs = []
    for row in range(NROW):
        there = row ^ ((y * NZH + z) * NCORE + core)
        pairs += [(row * NCOL + col, there * NCOL + col) for col in range(NCOL)]
    return lax.ppermute(value, ("row", "col"), pairs)


def in_vmem(kernel, results, operands, name, flops=MB, grant=8, **extra):
    spec = pl.BlockSpec(memory_space=pltpu.VMEM)
    outs = [shape if plain else pltpu.VMEM(shape.shape, shape.dtype) for shape, plain in results]
    out_specs = [pl.BlockSpec() if plain else spec for _, plain in results]
    return pl.pallas_call(
        kernel,
        in_specs=[spec] * len(operands),
        out_specs=out_specs,
        out_shape=outs,
        compiler_params=pltpu.CompilerParams(vmem_limit_bytes=grant * MB),
        cost_estimate=pl.CostEstimate(flops=flops, bytes_accessed=3 * MB, transcendentals=0),
        name=name,
        **extra,
    )(*[pltpu.with_memory_space_constraint(v, pltpu.VMEM) for v in operands])


def kept(shape, dtype):
    return jax.ShapeDtypeStruct(shape, dtype), False


def plain(shape, dtype):
    return jax.ShapeDtypeStruct(shape, dtype), True


def adjacency_kernel(place, where, masks, out, held, sems):
    count, slots = masks.shape[0], masks.shape[1]
    copies = [pltpu.make_async_copy(masks.at[j], held.at[j], sems.at[j]) for j in range(count)]
    for copy in copies:
        copy.start()
    for j, copy in enumerate(copies):
        cols = pl.ds(pl.multiple_of(place[j] * TILE, TILE), TILE)
        out[:, cols] = jnp.zeros((out.shape[0], TILE), BF16)
        copy.wait()
        for k in range(slots):
            at = pl.ds(pl.multiple_of(where[j * slots + k] * TILE, TILE), TILE)
            out[at, cols] = out[at, cols] + held[j, k].astype(F32).astype(BF16)


def adjacency(masks, place, where):
    count = masks.shape[0]
    return pl.pallas_call(
        adjacency_kernel,
        grid_spec=pltpu.PrefetchScalarGridSpec(
            num_scalar_prefetch=2,
            grid=(1,),
            in_specs=[pl.BlockSpec(memory_space=pl.ANY)],
            out_specs=pl.BlockSpec(memory_space=pltpu.VMEM),
            scratch_shapes=[pltpu.VMEM(masks.shape, masks.dtype), pltpu.SemaphoreType.DMA((count,))],
        ),
        out_shape=pltpu.VMEM((NCOL * TILE, count * TILE), BF16),
        compiler_params=pltpu.CompilerParams(vmem_limit_bytes=8 * MB),
        cost_estimate=pl.CostEstimate(flops=0, bytes_accessed=14 * MB, transcendentals=0),
        name="adjacency",
    )(place, where, pltpu.with_memory_space_constraint(masks, pltpu.HBM))


def gather_kernel(cores, dys, halves, adj, *refs):
    parts, start, out = refs[: len(halves) * len(cores)], None, refs[-1]
    if len(refs) > len(parts) + 1:
        start = refs[-2]
    half = parts[0].shape[1]
    depth = NZH * TILE
    rows = 2 * TILE
    for r in range(0, out.shape[0], rows):
        for n, h in enumerate(halves):
            cols = slice(h * half, (h + 1) * half)
            value = None if start is None else start[r : r + rows, cols].astype(F32)
            for i, core in enumerate(cores):
                at = [(core * NY + dy) * depth for dy in dys[h]]
                lhs = jnp.concatenate([adj[r : r + rows, a : a + depth] for a in at], axis=1)
                term = jnp.dot(lhs, parts[len(halves) * i + n][...], preferred_element_type=F32)
                value = term if value is None else value + term
            out[r : r + rows, cols] = value.astype(out.dtype)
        for h in set(range(2)) - set(halves):
            cols = slice(h * half, (h + 1) * half)
            out[r : r + rows, cols] = start[r : r + rows, cols].astype(out.dtype)


def gather_matmul(adj, parts, cores, dys, start, dtype, name, halves=(0, 1)):
    rows, width = adj.shape[0], 2 * parts[0].shape[1]
    operands = [adj, *parts] + ([] if start is None else [start])
    kernel = functools.partial(gather_kernel, cores, dys, halves)
    return in_vmem(kernel, [kept((rows, width), dtype)], operands, name)[0]


def node_kernel(parts, base, degf_row, w_neigh, cotangent, grad, scaled_t, out):
    total = parts[0:TILE, :].astype(F32)
    for i in range(1, NCOL):
        total = total + parts[i * TILE : (i + 1) * TILE, :].astype(F32)
    degf_col = jnp.broadcast_to(degf_row[...], (TILE, TILE)).T[:, :1]
    mean = (total / degf_col).astype(BF16)
    pre = base[...] + jnp.dot(mean, w_neigh[...], preferred_element_type=F32)
    sig = jax.nn.sigmoid(pre)
    out[...] = (pre * sig).astype(BF16)
    slope = sig * (1.0 + pre * (1.0 - sig))
    grad_pre = (cotangent[...].astype(F32) * slope).astype(BF16)
    grad[...] = grad_pre
    proj_t = lax.dot_general(w_neigh[...], grad_pre, (((1,), (1,)), ((), ())), preferred_element_type=F32)
    scaled = (proj_t / degf_row[...]).astype(BF16)
    for i in range(NCOL):
        scaled_t[i, :, :] = scaled


def node_step(parts, base, degf_row, w_neigh, cotangent):
    rows, width = cotangent.shape
    results = [kept((rows, width), BF16), kept((NCOL, width, rows), BF16), plain((rows, width), BF16)]
    operands = (parts, base, degf_row, w_neigh, cotangent)
    return in_vmem(node_kernel, results, operands, "node_step", 4 * rows * width * width)


def spread_kernel(core, pick, parts, adj, out):
    depth = NZH * TILE
    half = out.shape[1]
    for h, steps in enumerate(STEPS):
        lhs = jnp.concatenate([parts[i, h * half : (h + 1) * half, :] for i in range(NCOL)], axis=1)
        for n, dy in enumerate(pick(*steps)):
            at = (core * NY + dy) * depth
            value = jnp.dot(lhs, adj[:, at : at + depth], preferred_element_type=F32)
            out[h, :, n * depth : (n + 1) * depth] = value.astype(BF16)


def spread_matmul(parts, adj, core, pick, name):
    shape = (2, parts.shape[1] // 2, 2 * NZH * TILE)
    return in_vmem(functools.partial(spread_kernel, core, pick), [kept(shape, BF16)], (parts, adj), name)[0]


def goes(k1, k2):
    return k2, k1 ^ k2


def stays(k1, k2):
    return 0, k1


def total(refs):
    value = refs[0][...].astype(F32)
    for ref in refs[1:]:
        value = value + ref[...].astype(F32)
    return value


def both_halves_kernel(mine, theirs, *outs):
    for h, out in enumerate(outs):
        out[...] = (mine[h].astype(F32) + theirs[h].astype(F32)).astype(BF16)


def both_halves(mine, theirs):
    return in_vmem(both_halves_kernel, [kept(mine.shape[1:], BF16)] * 2, (mine, theirs), "both_halves")


def first_split_kernel(h, mine, theirs, got, stay, go):
    value = mine[h].astype(F32) + theirs[h].astype(F32) + got[...].astype(F32)
    depth = stay.shape[1]
    stay[...] = value[:, :depth]
    go[...] = value[:, depth:].astype(BF16)


def first_split(h, mine, theirs, got, name):
    shape = (got.shape[0], got.shape[1] // 2)
    results = [kept(shape, F32), kept(shape, BF16)]
    return in_vmem(functools.partial(first_split_kernel, h), results, (mine, theirs, got), name)


def split_kernel(stays, goes, *refs):
    value = total(refs[:-2])
    for out, tiles in zip(refs[-2:], (stays, goes)):
        for i, tile in enumerate(tiles):
            part = value[:, tile * TILE : (tile + 1) * TILE]
            out[:, i * TILE : (i + 1) * TILE] = part.astype(out.dtype)


def add_split(values, stays, goes, name):
    rows = values[0].shape[0]
    results = [kept((rows, len(stays) * TILE), F32), kept((rows, len(goes) * TILE), BF16)]
    return in_vmem(functools.partial(split_kernel, stays, goes), results, values, name)


def last_kernel(*refs):
    own, out = refs[-2:]
    back = jnp.concatenate([total(refs[0:2]), total(refs[2:4])], axis=0)
    out[...] = (own[...] + back.T).astype(BF16)


def last_sum(values, own):
    return in_vmem(last_kernel, [plain(own.shape, BF16)], (*values, own), "last_sum")[0]


def body(features, degrees, tile_rows, tile_masks, w_self, w_neigh, bias, cotangent):
    half = features.shape[1] // 2
    row = lax.axis_index("row").astype(jnp.int32)

    differ = jnp.arange(NROW, dtype=jnp.int32) ^ row
    place = (differ % NCORE) * CHIPS + differ // NCORE
    where = tile_rows[0, 0].reshape(-1)
    degf_row = degrees.astype(F32)[None, :]
    base = jnp.dot(features, w_self, preferred_element_type=F32) + bias[None, :]

    chunks = [features[:, :half], features[:, half:]]
    firsts = [flip(v, z=k1) for v, (k1, _) in zip(chunks, STEPS)]
    pairs = [jnp.concatenate([v, r], axis=0) for v, r in zip(chunks, firsts)]
    seconds = [flip(v, z=k2) for v, (_, k2) in zip(pairs, STEPS)]
    adj = adjacency(tile_masks[0, 0], place, where)
    planes = []
    for v, first, second, (k1, k2) in zip(chunks, firsts, seconds, STEPS):
        tiles = {0: v, k1: first, k2: second[:TILE], k1 ^ k2: second[TILE:]}
        planes.append(jnp.concatenate([tiles[i] for i in range(NZH)], axis=0))
    thirds = [flip(v, y=k1) for v, (k1, _) in zip(planes, STEPS)]
    *thirds, adj, base, degf_row = lax.optimization_barrier((*thirds, adj, base, degf_row))
    near = [jnp.concatenate([v, r], axis=0) for v, r in zip(planes, thirds)]
    far = [flip(v, y=k2) for v, (_, k2) in zip(near, STEPS)]
    first, second = [(0, k1) for k1, _ in STEPS], [(k2, k1 ^ k2) for k1, k2 in STEPS]
    near = near + [flip(v, core=1) for v in near]
    part = gather_matmul(adj, near, (0, 1), first, None, F32, "gather_near")
    far[0], part = lax.optimization_barrier((far[0], part))
    other = [flip(v, core=1) for v in far]
    part = gather_matmul(adj, far, (0,), second, part, F32, "gather_far")
    other[0], part = lax.optimization_barrier((other[0], part))
    part = gather_matmul(adj, other[:1], (1,), second, part, F32, "gather_far_first", (0,))
    other[1], part = lax.optimization_barrier((other[1], part))
    summed = gather_matmul(adj, other[1:], (1,), second, part, BF16, "gather_far_second", (1,))

    arrived = lax.all_to_all(summed, "col", 0, 0, tiled=True)
    grad_pre, scaled_t, output = node_step(arrived, base, degf_row, w_neigh, cotangent)

    table = lax.all_to_all(scaled_t, "col", 0, 0, tiled=True)
    own = lax.dot_general(grad_pre, w_self, (((1,), (1,)), ((), ())), preferred_element_type=F32)
    send_in = flip(spread_matmul(table, adj, 1, goes, "spread_go_other"), core=1)
    send = spread_matmul(table, adj, 0, goes, "spread_go")
    keep_out = spread_matmul(table, adj, 1, stays, "spread_stay_other")
    send_in, send, keep_out = lax.optimization_barrier((send_in, send, keep_out))
    sums = list(both_halves(send, send_in))
    sums[0], keep_out, table = lax.optimization_barrier((sums[0], keep_out, table))
    keep_in = flip(keep_out, core=1)
    keep = spread_matmul(table, adj, 0, stays, "spread_stay")

    ends = []
    for h, (value, (k1, k2)) in enumerate(zip(sums, STEPS)):
        got = flip(value, y=k2)
        stay, go = first_split(h, keep, keep_in, got, "add_y1")
        got = flip(go, y=k1)
        stay, go = add_split((stay, got), (0, k1), (k2, k1 ^ k2), "add_y2")
        got = flip(go, z=k2)
        stay, go = add_split((stay, got), (0,), (1,), "add_z1")
        ends += [stay, flip(go, z=k1)]
    grad_features = last_sum(ends, own)
    return output, grad_features


def solution(mesh):
    both = P(("row", "col"), None)
    return jax.shard_map(
        body,
        mesh=mesh,
        in_specs=(
            both,
            P(("row", "col")),
            P("row", "col", None, None),
            P("row", "col", None, None, None, None),
            P(),
            P(),
            P(),
            both,
        ),
        out_specs=(both, both),
        check_vma=False,
    )
```

```python
import functools

import jax
import jax.numpy as jnp
from jax import lax
from jax.experimental import pallas as pl
from jax.experimental.pallas import tpu as pltpu
from jax.sharding import PartitionSpec as P

NY, NZH, NCORE, NX, NZL = 4, 4, 2, 4, 2
NROW, NCOL = NY * NZH * NCORE, NX * NZL
CHIPS = NY * NZH
STEPS = ((1, 3), (3, 1))
TILE = 128
BF16 = jnp.bfloat16
F32 = jnp.float32
MB = 1024 * 1024


def flip(value, y=0, z=0, core=0):
    pairs = []
    for row in range(NROW):
        there = row ^ ((y * NZH + z) * NCORE + core)
        pairs += [(row * NCOL + col, there * NCOL + col) for col in range(NCOL)]
    return lax.ppermute(value, ("row", "col"), pairs)


def in_vmem(kernel, results, operands, name, flops=MB, grant=8, **extra):
    spec = pl.BlockSpec(memory_space=pltpu.VMEM)
    outs = [shape if plain else pltpu.VMEM(shape.shape, shape.dtype) for shape, plain in results]
    out_specs = [pl.BlockSpec() if plain else spec for _, plain in results]
    return pl.pallas_call(
        kernel,
        in_specs=[spec] * len(operands),
        out_specs=out_specs,
        out_shape=outs,
        compiler_params=pltpu.CompilerParams(vmem_limit_bytes=grant * MB),
        cost_estimate=pl.CostEstimate(flops=flops, bytes_accessed=3 * MB, transcendentals=0),
        name=name,
        **extra,
    )(*[pltpu.with_memory_space_constraint(v, pltpu.VMEM) for v in operands])


def kept(shape, dtype):
    return jax.ShapeDtypeStruct(shape, dtype), False


def plain(shape, dtype):
    return jax.ShapeDtypeStruct(shape, dtype), True


def adjacency_kernel(place, where, masks, out, held, sems):
    count, slots = masks.shape[0], masks.shape[1]
    copies = [pltpu.make_async_copy(masks.at[j], held.at[j], sems.at[j]) for j in range(count)]
    for copy in copies:
        copy.start()
    for j, copy in enumerate(copies):
        cols = pl.ds(pl.multiple_of(place[j] * TILE, TILE), TILE)
        out[:, cols] = jnp.zeros((out.shape[0], TILE), BF16)
        copy.wait()
        for k in range(slots):
            at = pl.ds(pl.multiple_of(where[j * slots + k] * TILE, TILE), TILE)
            out[at, cols] = out[at, cols] + held[j, k].astype(F32).astype(BF16)


def adjacency(masks, place, where):
    count = masks.shape[0]
    return pl.pallas_call(
        adjacency_kernel,
        grid_spec=pltpu.PrefetchScalarGridSpec(
            num_scalar_prefetch=2,
            grid=(1,),
            in_specs=[pl.BlockSpec(memory_space=pl.ANY)],
            out_specs=pl.BlockSpec(memory_space=pltpu.VMEM),
            scratch_shapes=[pltpu.VMEM(masks.shape, masks.dtype), pltpu.SemaphoreType.DMA((count,))],
        ),
        out_shape=pltpu.VMEM((NCOL * TILE, count * TILE), BF16),
        compiler_params=pltpu.CompilerParams(vmem_limit_bytes=8 * MB),
        cost_estimate=pl.CostEstimate(flops=0, bytes_accessed=14 * MB, transcendentals=0),
        name="adjacency",
    )(place, where, pltpu.with_memory_space_constraint(masks, pltpu.HBM))


def gather_kernel(cores, dys, halves, adj, *refs):
    parts, start, out = refs[: len(halves) * len(cores)], None, refs[-1]
    if len(refs) > len(parts) + 1:
        start = refs[-2]
    half = parts[0].shape[1]
    depth = NZH * TILE
    rows = 2 * TILE
    for r in range(0, out.shape[0], rows):
        for n, h in enumerate(halves):
            cols = slice(h * half, (h + 1) * half)
            value = None if start is None else start[r : r + rows, cols].astype(F32)
            for i, core in enumerate(cores):
                at = [(core * NY + dy) * depth for dy in dys[h]]
                lhs = jnp.concatenate([adj[r : r + rows, a : a + depth] for a in at], axis=1)
                term = jnp.dot(lhs, parts[len(halves) * i + n][...], preferred_element_type=F32)
                value = term if value is None else value + term
            out[r : r + rows, cols] = value.astype(out.dtype)
        for h in set(range(2)) - set(halves):
            cols = slice(h * half, (h + 1) * half)
            out[r : r + rows, cols] = start[r : r + rows, cols].astype(out.dtype)


def gather_matmul(adj, parts, cores, dys, start, dtype, name, halves=(0, 1)):
    rows, width = adj.shape[0], 2 * parts[0].shape[1]
    operands = [adj, *parts] + ([] if start is None else [start])
    kernel = functools.partial(gather_kernel, cores, dys, halves)
    return in_vmem(kernel, [kept((rows, width), dtype)], operands, name)[0]


def node_kernel(parts, base, degf_row, w_neigh, cotangent, grad, scaled_t, before):
    total = parts[0:TILE, :].astype(F32)
    for i in range(1, NCOL):
        total = total + parts[i * TILE : (i + 1) * TILE, :].astype(F32)
    degf_col = jnp.broadcast_to(degf_row[...], (TILE, TILE)).T[:, :1]
    mean = (total / degf_col).astype(BF16)
    pre = base[...] + jnp.dot(mean, w_neigh[...], preferred_element_type=F32)
    sig = jax.nn.sigmoid(pre)
    before[...] = pre
    slope = sig * (1.0 + pre * (1.0 - sig))
    grad_pre = (cotangent[...].astype(F32) * slope).astype(BF16)
    grad[...] = grad_pre
    proj_t = lax.dot_general(w_neigh[...], grad_pre, (((1,), (1,)), ((), ())), preferred_element_type=F32)
    scaled = (proj_t / degf_row[...]).astype(BF16)
    for i in range(NCOL):
        scaled_t[i, :, :] = scaled


def node_step(parts, base, degf_row, w_neigh, cotangent):
    rows, width = cotangent.shape
    results = [kept((rows, width), BF16), kept((NCOL, width, rows), BF16), kept((rows, width), F32)]
    operands = (parts, base, degf_row, w_neigh, cotangent)
    return in_vmem(node_kernel, results, operands, "node_step", 4 * rows * width * width)


def silu_kernel(pre, out):
    out[...] = (pre[...] * jax.nn.sigmoid(pre[...])).astype(BF16)


def silu(pre):
    return in_vmem(silu_kernel, [plain(pre.shape, BF16)], (pre,), "silu")[0]


def spread_kernel(core, pick, parts, adj, out):
    depth = NZH * TILE
    half = out.shape[1]
    for h, steps in enumerate(STEPS):
        lhs = jnp.concatenate([parts[i, h * half : (h + 1) * half, :] for i in range(NCOL)], axis=1)
        for n, dy in enumerate(pick(*steps)):
            at = (core * NY + dy) * depth
            value = jnp.dot(lhs, adj[:, at : at + depth], preferred_element_type=F32)
            out[h, :, n * depth : (n + 1) * depth] = value.astype(BF16)


def spread_matmul(parts, adj, core, pick, name):
    shape = (2, parts.shape[1] // 2, 2 * NZH * TILE)
    return in_vmem(functools.partial(spread_kernel, core, pick), [kept(shape, BF16)], (parts, adj), name)[0]


def goes(k1, k2):
    return k2, k1 ^ k2


def stays(k1, k2):
    return 0, k1


def total(refs):
    value = refs[0][...].astype(F32)
    for ref in refs[1:]:
        value = value + ref[...].astype(F32)
    return value


def both_halves_kernel(mine, theirs, *outs):
    for h, out in enumerate(outs):
        out[...] = (mine[h].astype(F32) + theirs[h].astype(F32)).astype(BF16)


def both_halves(mine, theirs):
    return in_vmem(both_halves_kernel, [kept(mine.shape[1:], BF16)] * 2, (mine, theirs), "both_halves")


def first_split_kernel(h, mine, theirs, got, stay, go):
    value = mine[h].astype(F32) + theirs[h].astype(F32) + got[...].astype(F32)
    depth = stay.shape[1]
    stay[...] = value[:, :depth]
    go[...] = value[:, depth:].astype(BF16)


def first_split(h, mine, theirs, got, name):
    shape = (got.shape[0], got.shape[1] // 2)
    results = [kept(shape, F32), kept(shape, BF16)]
    return in_vmem(functools.partial(first_split_kernel, h), results, (mine, theirs, got), name)


def split_kernel(stays, goes, *refs):
    value = total(refs[:-2])
    for out, tiles in zip(refs[-2:], (stays, goes)):
        for i, tile in enumerate(tiles):
            part = value[:, tile * TILE : (tile + 1) * TILE]
            out[:, i * TILE : (i + 1) * TILE] = part.astype(out.dtype)


def add_split(values, stays, goes, name):
    rows = values[0].shape[0]
    results = [kept((rows, len(stays) * TILE), F32), kept((rows, len(goes) * TILE), BF16)]
    return in_vmem(functools.partial(split_kernel, stays, goes), results, values, name)


def last_kernel(*refs):
    own, out = refs[-2:]
    back = jnp.concatenate([total(refs[0:2]), total(refs[2:4])], axis=0)
    out[...] = (own[...] + back.T).astype(BF16)


def last_sum(values, own):
    return in_vmem(last_kernel, [plain(own.shape, BF16)], (*values, own), "last_sum")[0]


def body(features, degrees, tile_rows, tile_masks, w_self, w_neigh, bias, cotangent):
    half = features.shape[1] // 2
    row = lax.axis_index("row").astype(jnp.int32)

    differ = jnp.arange(NROW, dtype=jnp.int32) ^ row
    place = (differ % NCORE) * CHIPS + differ // NCORE
    where = tile_rows[0, 0].reshape(-1)
    degf_row = degrees.astype(F32)[None, :]
    base = jnp.dot(features, w_self, preferred_element_type=F32) + bias[None, :]

    chunks = [features[:, :half], features[:, half:]]
    firsts = [flip(v, z=k1) for v, (k1, _) in zip(chunks, STEPS)]
    pairs = [jnp.concatenate([v, r], axis=0) for v, r in zip(chunks, firsts)]
    seconds = [flip(v, z=k2) for v, (_, k2) in zip(pairs, STEPS)]
    adj = adjacency(tile_masks[0, 0], place, where)
    planes = []
    for v, first, second, (k1, k2) in zip(chunks, firsts, seconds, STEPS):
        tiles = {0: v, k1: first, k2: second[:TILE], k1 ^ k2: second[TILE:]}
        planes.append(jnp.concatenate([tiles[i] for i in range(NZH)], axis=0))
    thirds = [flip(v, y=k1) for v, (k1, _) in zip(planes, STEPS)]
    *thirds, adj, base, degf_row = lax.optimization_barrier((*thirds, adj, base, degf_row))
    near = [jnp.concatenate([v, r], axis=0) for v, r in zip(planes, thirds)]
    far = [flip(v, y=k2) for v, (_, k2) in zip(near, STEPS)]
    first, second = [(0, k1) for k1, _ in STEPS], [(k2, k1 ^ k2) for k1, k2 in STEPS]
    near = near + [flip(v, core=1) for v in near]
    part = gather_matmul(adj, near, (0, 1), first, None, F32, "gather_near")
    far[0], part = lax.optimization_barrier((far[0], part))
    other = [flip(v, core=1) for v in far]
    part = gather_matmul(adj, far, (0,), second, part, F32, "gather_far")
    other[0], part = lax.optimization_barrier((other[0], part))
    part = gather_matmul(adj, other[:1], (1,), second, part, F32, "gather_far_first", (0,))
    other[1], part = lax.optimization_barrier((other[1], part))
    summed = gather_matmul(adj, other[1:], (1,), second, part, BF16, "gather_far_second", (1,))

    arrived = lax.all_to_all(summed, "col", 0, 0, tiled=True)
    grad_pre, scaled_t, pre = node_step(arrived, base, degf_row, w_neigh, cotangent)

    table = lax.all_to_all(scaled_t, "col", 0, 0, tiled=True)
    own = lax.dot_general(grad_pre, w_self, (((1,), (1,)), ((), ())), preferred_element_type=F32)
    send_in = flip(spread_matmul(table, adj, 1, goes, "spread_go_other"), core=1)
    send = spread_matmul(table, adj, 0, goes, "spread_go")
    keep_out = spread_matmul(table, adj, 1, stays, "spread_stay_other")
    send_in, send, keep_out = lax.optimization_barrier((send_in, send, keep_out))
    sums = list(both_halves(send, send_in))
    sums[0], keep_out, table, pre = lax.optimization_barrier((sums[0], keep_out, table, pre))
    output = silu(pre)
    keep_in = flip(keep_out, core=1)
    keep = spread_matmul(table, adj, 0, stays, "spread_stay")

    ends = []
    for h, (value, (k1, k2)) in enumerate(zip(sums, STEPS)):
        got = flip(value, y=k2)
        stay, go = first_split(h, keep, keep_in, got, "add_y1")
        got = flip(go, y=k1)
        stay, go = add_split((stay, got), (0, k1), (k2, k1 ^ k2), "add_y2")
        got = flip(go, z=k2)
        stay, go = add_split((stay, got), (0,), (1,), "add_z1")
        ends += [stay, flip(go, z=k1)]
    grad_features = last_sum(ends, own)
    return output, grad_features


def solution(mesh):
    both = P(("row", "col"), None)
    return jax.shard_map(
        body,
        mesh=mesh,
        in_specs=(
            both,
            P(("row", "col")),
            P("row", "col", None, None),
            P("row", "col", None, None, None, None),
            P(),
            P(),
            P(),
            both,
        ),
        out_specs=(both, both),
        check_vma=False,
    )
```
